256 devices in a mesh: ens: 4 (over y), band: 64 (over z, x, core).
Axes of the slice: x: 4, y: 4, z: 8, core: 2. Of those that a mesh axis runs over, the one named last changes fastest.
Arguments:
- spectral_state: bfloat16 [1536, 384, 256], P(('ens', 'band')), parts along dimension 0, may hold values from -0.29882812 to 0.29882812
- lat_basis: bfloat16 [384, 640, 384], P('band'), may hold values from -0.3125 to 0.3125
- quad_weight: float32 [640], P('band'), may hold values from 0.5 to 2
- wave_of_slot: int32 [384], replicated, may hold values from 0 to 383, each once
- dest_owner: int32 [640, 1440], P('band'), may hold values from 0 to 63, as said below
- dest_slot: int32 [640, 1440], P('band'), may hold values from 0 to 14399, as said below
- surface: bfloat16 [921600, 128], P('band'), may hold values from -6 to 6
- in_weight: bfloat16 [128, 256], replicated, may hold values from -0.5 to 0.5
- surface_weight: bfloat16 [128, 256], replicated, may hold values from -0.5 to 0.5
- in_bias: float32 [256], replicated, may hold values from -3 to 3
- mid_weight: bfloat16 [256, 256], replicated, may hold values from -0.375 to 0.375
- mid_bias: float32 [256], replicated, may hold values from -3 to 3
- out_weight: bfloat16 [256, 128], replicated, may hold values from -0.375 to 0.375
Outputs:
- spectral_tendency: float32 [1536, 384, 256], P(('ens', 'band')), parts along dimension 0
The draws below stay inside these ranges and needn't reach their ends.
There are 4 independent parts, one for each index of `ens`. The reference program is written for one: setup_inputs(seed, part) draws one part's arguments, and reference() takes and returns one part's arrays. A program takes and returns all parts, laid end to end along the dimension named above; an argument that names none is the same for every part. Nothing has to cross between parts.
Inputs may be any that keep to these rules, and one draw needn't show every extreme that they name: `wave_of_slot`: each number once. `dest_owner`: the columns of each band of 10 latitudes are dealt in turn to the owners along a Hilbert curve over the grid; every band gives exactly 225 columns to each owner. `dest_slot`: each owner's 14400 columns have different slots.
All inputs are finite; a program needn't handle non-finite values.
Results may differ from the reference program's by a relative error of at most 0.009.
Values may be sent and summed in bfloat16 or wider, within the bound.
No kernel may reach another device: no remote copies, remote signals or barrier semaphores. Data moves between devices by JAX's collectives and lax.ppermute only.
A program may use at most 128 MiB of HBM per device.

```python
import math
import jax
import jax.numpy as jnp
from jax import lax

NLAT = 640
NLON = 1440
MW = 384
NDEG = 384
HID = 256
FORC = 128
F = 128
CF = 256
COLS_DEV = 14400
N_BAND = 64


def hilbert_index(across, down, bits):
    side = 2 ** bits
    distance = jnp.zeros_like(across)
    level = side // 2
    while level > 0:
        right = across & level > 0
        upper = down & level > 0
        quadrant = jnp.where(right, 3, 0).astype(jnp.int32) ^ upper.astype(jnp.int32)
        distance = distance + level * level * quadrant
        mirror = jnp.logical_and(jnp.logical_not(upper), right)
        across_new = jnp.where(mirror, side - 1 - across, across)
        down_new = jnp.where(mirror, side - 1 - down, down)
        swapped = jnp.logical_not(upper)
        across = jnp.where(swapped, down_new, across_new)
        down = jnp.where(swapped, across_new, down_new)
        level = level // 2
    return distance


def hilbert_layout(key):
    offset_draw = jax.random.randint(jax.random.fold_in(key, 101), (), 0, NLON)
    band_offsets = jax.random.randint(jax.random.fold_in(key, 102), (N_BAND,), 0, N_BAND)
    bits = (max(NLAT, NLON) - 1).bit_length()
    latitude = jnp.arange(NLAT, dtype=jnp.int32)[:, None] * jnp.ones((1, NLON), jnp.int32)
    longitude = (jnp.arange(NLON, dtype=jnp.int32)[None, :] + offset_draw) % NLON
    longitude = longitude * jnp.ones((NLAT, 1), jnp.int32)
    distance = hilbert_index(longitude, latitude, bits)
    per_band = distance.reshape(N_BAND, COLS_DEV)
    visits = jnp.argsort(per_band, axis=1).astype(jnp.int32)
    band_ids = jnp.arange(N_BAND, dtype=jnp.int32)[:, None] * jnp.ones((1, COLS_DEV), jnp.int32)
    ranks = jnp.zeros((N_BAND, COLS_DEV), jnp.int32).at[band_ids, visits].set(jnp.arange(COLS_DEV, dtype=jnp.int32)[None, :] * jnp.ones((N_BAND, 1), jnp.int32))
    owners = (ranks + band_offsets[:, None]) % N_BAND
    sort_keys = (owners * 4 ** bits + per_band).reshape(-1)
    arrange = jnp.argsort(sort_keys).astype(jnp.int32)
    positions = jnp.zeros((NLAT * NLON,), jnp.int32).at[arrange].set(jnp.arange(NLAT * NLON, dtype=jnp.int32))
    slots = positions - owners.reshape(-1) * COLS_DEV
    return (owners.reshape(NLAT, NLON), slots.reshape(NLAT, NLON))


def draw_dest_owner(key, part):
    shared = hilbert_layout(key)
    return shared[0]


def draw_dest_slot(key, part):
    shared = hilbert_layout(key)
    return shared[1]


def shard_levels(key, shape, pieces, low, largest):
    def one(dim, parts):
        heights = jax.random.uniform(jax.random.fold_in(jax.random.fold_in(key, 6), dim), (parts,), jnp.float32, low / len(pieces), largest / len(pieces))
        return jnp.repeat(jnp.exp(heights), shape[dim] // parts).reshape((-1,) + (1,) * (len(shape) - dim - 1))

    loudness = one(*pieces[0])
    for cut in pieces[1:]:
        loudness = loudness * one(*cut)
    return loudness


def centred(stream_key, dims, scale, most, cuts=(), kind=jnp.bfloat16):
    factor_of = shard_levels(stream_key, dims, cuts, -0.22, 0.18) if cuts else 1.0
    result = jax.random.normal(stream_key, dims, jnp.float32) * scale * factor_of
    return jnp.minimum(jnp.maximum(result, -most), most).astype(kind)


def setup_inputs(seed: int = 0, part: int = 0) -> dict:
    arg_keys = jax.random.split(jax.random.key(seed), 14)
    part_splits = jax.random.split(jax.random.fold_in(arg_keys[13], part), 14)
    spectral_state = centred(part_splits[0], (MW, NDEG, CF), 0.05, 0.29882812, ((0, 64),))
    lat_basis = centred(arg_keys[1], (MW, NLAT, NDEG), NDEG ** -0.5, 0.3125, ((0, 64),))
    quad_weight = jnp.clip(jnp.exp(math.log(2.0) - 1.3862944 * jax.random.uniform(arg_keys[2], (NLAT,), jnp.float32) ** shard_levels(arg_keys[2], (NLAT,), ((0, 64),), -0.2, 0.2)), 0.5, 2.0)
    wave_of_slot = jax.random.permutation(arg_keys[3], MW).astype(jnp.int32)
    dest_owner = draw_dest_owner(jax.random.fold_in(arg_keys[13], 71), part)
    dest_slot = draw_dest_slot(jax.random.fold_in(arg_keys[13], 71), part)
    surface = centred(arg_keys[6], (NLAT * NLON, FORC), 1.0, 6.0, ((0, 64),))
    in_weight = centred(arg_keys[7], (F, HID), F ** -0.5, 0.5)
    surface_weight = centred(arg_keys[8], (FORC, HID), FORC ** -0.5, 0.5)
    in_bias = centred(arg_keys[9], (HID,), 0.5, 3.0, (), jnp.float32)
    mid_weight = centred(arg_keys[10], (HID, HID), HID ** -0.5, 0.375)
    mid_bias = centred(arg_keys[11], (HID,), 0.5, 3.0, (), jnp.float32)
    out_weight = centred(arg_keys[12], (HID, F), HID ** -0.5, 0.375)
    return {"spectral_state": spectral_state, "lat_basis": lat_basis, "quad_weight": quad_weight, "wave_of_slot": wave_of_slot, "dest_owner": dest_owner, "dest_slot": dest_slot, "surface": surface, "in_weight": in_weight, "surface_weight": surface_weight, "in_bias": in_bias, "mid_weight": mid_weight, "mid_bias": mid_bias, "out_weight": out_weight}


def fourier_table(wave_of_slot, longitudes):
    wavenumbers = wave_of_slot.astype(jnp.int32) + 1
    positions = jnp.arange(longitudes, dtype=jnp.int32)
    phases = wavenumbers[:, None] * positions[None, :] % longitudes
    angles = phases.astype(jnp.float32) * (2.0 * math.pi / longitudes)
    return jnp.stack([jnp.cos(angles), -jnp.sin(angles)]).astype(jnp.bfloat16)

def column_model(columns, surface_rows, in_weight, surface_weight, in_bias, mid_weight, mid_bias, out_weight):
    first_layer = jnp.dot(columns, in_weight, preferred_element_type=jnp.float32)
    first_layer = first_layer + jnp.dot(surface_rows, surface_weight, preferred_element_type=jnp.float32) + in_bias
    first_layer = jax.nn.silu(first_layer).astype(jnp.bfloat16)
    second_layer = jnp.dot(first_layer, mid_weight, preferred_element_type=jnp.float32) + mid_bias
    second_layer = jax.nn.silu(second_layer).astype(jnp.bfloat16)
    return jnp.dot(second_layer, out_weight, preferred_element_type=jnp.float32).astype(jnp.bfloat16)

def reference(spectral_state, lat_basis, quad_weight, wave_of_slot, dest_owner, dest_slot, surface, in_weight, surface_weight, in_bias, mid_weight, mid_bias, out_weight):
    fourier_tab = fourier_table(wave_of_slot, NLON).astype(jnp.float32)
    basis_wide = lat_basis.astype(jnp.float32)
    fourier = jnp.einsum('sln,snc->slc', basis_wide, spectral_state.astype(jnp.float32)).astype(jnp.bfloat16)
    lat_rows = NLAT // N_BAND
    by_band = fourier.reshape(MW, N_BAND, lat_rows, 2, F).transpose(1, 0, 2, 3, 4)
    places = (dest_owner * COLS_DEV + dest_slot).reshape(N_BAND, lat_rows * NLON)
    weights = quad_weight.reshape(N_BAND, lat_rows)
    factor = math.sqrt(2.0 / NLON)

    def one_band(inputs):
        coefficients, place_ids, weight = inputs
        grid_state = jnp.einsum('slcf,csx->lxf', coefficients.astype(jnp.float32), fourier_tab).astype(jnp.bfloat16)
        rows_here = surface[place_ids]
        tendency = column_model(grid_state.reshape(-1, F), rows_here, in_weight, surface_weight, in_bias, mid_weight, mid_bias, out_weight)
        tendency = tendency.reshape(lat_rows, NLON, F).astype(jnp.float32)
        spectrum = jnp.einsum('lxf,csx->slcf', tendency, fourier_tab)
        spectrum = spectrum * (factor * weight)[None, :, None, None]
        return spectrum.astype(jnp.bfloat16)
    per_band = lax.map(one_band, (by_band, places, weights))
    spectrum = per_band.transpose(1, 0, 2, 3, 4).reshape(MW, NLAT, 2 * F)
    return jnp.einsum('sln,slc->snc', basis_wide, spectrum.astype(jnp.float32))
```

```python
import functools
import math

import jax
import jax.numpy as jnp
from jax import lax
from jax.experimental import pallas as pl
from jax.experimental.pallas import tpu as pltpu
from jax.sharding import PartitionSpec as P

VMEM_BYTES = 48 * 1024 * 1024


def whole(shape):
    zeros = (0,) * len(shape)
    return pl.BlockSpec(shape, lambda *_: zeros)


def fourier_kernel(basis_ref, state_ref, out_ref, wide):
    slots, lats, features = pl.num_programs(0), basis_ref.shape[1], out_ref.shape[1]
    slot = pl.program_id(0)
    per_lat = out_ref.shape[0] // lats
    found = jnp.dot(basis_ref[0], state_ref[0], preferred_element_type=jnp.float32)
    for k in range(2):
        wide[pl.ds(2 * slot + k, lats, per_lat), :] = found[:, k * features : (k + 1) * features]

    @pl.when(slot == slots - 1)
    def _():
        out_ref[...] = wide[...].astype(out_ref.dtype)


def to_latitudes(lat_basis, spectral_state):
    slots, lats, degrees = lat_basis.shape
    features = spectral_state.shape[2] // 2
    rows = lats * slots * 2
    return pl.pallas_call(
        fourier_kernel,
        grid=(slots,),
        in_specs=[
            pl.BlockSpec((1, lats, degrees), lambda s: (s, 0, 0)),
            pl.BlockSpec((1, degrees, 2 * features), lambda s: (s, 0, 0)),
        ],
        out_specs=whole((rows, features)),
        out_shape=jax.ShapeDtypeStruct((rows, features), jnp.bfloat16),
        scratch_shapes=[pltpu.VMEM((rows, features), jnp.float32)],
        compiler_params=pltpu.CompilerParams(vmem_limit_bytes=VMEM_BYTES),
        cost_estimate=pl.CostEstimate(
            flops=2 * slots * lats * degrees * 2 * features,
            bytes_accessed=2 * (lat_basis.size + spectral_state.size + rows * features),
            transcendentals=0,
        ),
        name="to_latitudes",
    )(lat_basis, spectral_state)


def degrees_kernel(basis_ref, rows_ref, out_ref, wide):
    lats = basis_ref.shape[1]
    slot = pl.program_id(0)
    per_lat = rows_ref.shape[0] // lats

    @pl.when(slot == 0)
    def _():
        wide[...] = rows_ref[...].astype(jnp.float32)

    spectrum = jnp.concatenate(
        [wide[pl.ds(2 * slot + k, lats, per_lat), :].astype(jnp.bfloat16) for k in range(2)],
        axis=1,
    )
    out_ref[0] = lax.dot_general(
        basis_ref[0], spectrum, (((0,), (0,)), ((), ())), preferred_element_type=jnp.float32
    )


def to_degrees(lat_basis, rows):
    slots, lats, degrees = lat_basis.shape
    features = rows.shape[1]
    return pl.pallas_call(
        degrees_kernel,
        grid=(slots,),
        in_specs=[
            pl.BlockSpec((1, lats, degrees), lambda s: (s, 0, 0)),
            whole(rows.shape),
        ],
        out_specs=pl.BlockSpec((1, degrees, 2 * features), lambda s: (s, 0, 0)),
        out_shape=jax.ShapeDtypeStruct((slots, degrees, 2 * features), jnp.float32),
        scratch_shapes=[pltpu.VMEM(rows.shape, jnp.float32)],
        compiler_params=pltpu.CompilerParams(vmem_limit_bytes=VMEM_BYTES),
        cost_estimate=pl.CostEstimate(
            flops=2 * slots * lats * degrees * 2 * features,
            bytes_accessed=2 * (lat_basis.size + rows.size) + 8 * slots * degrees * features,
            transcendentals=0,
        ),
        name="to_degrees",
    )(lat_basis, rows)


def angle_parts(waves, step, count, quarter, longitudes, axis):
    positions = jnp.arange(count, dtype=jnp.int32) * step
    shape = (-1, 1) if axis == 1 else (1, -1)
    phases = waves.reshape(shape) * positions.reshape(shape[::-1])
    phases = (phases + quarter.reshape(shape)) % longitudes
    angles = phases.astype(jnp.float32) * (2.0 * math.pi / longitudes)
    return jnp.cos(angles), jnp.sin(angles)


def table_kernel(hi_cos, hi_sin, lo_cos, lo_sin, hi_cos_t, hi_sin_t, lo_cos_t, lo_sin_t, out, out_t):
    longitudes = out.shape[1]
    width = lo_cos.shape[1]
    for a in range(hi_cos.shape[1]):
        size = min(width, longitudes - a * width)
        block = hi_cos[:, a : a + 1] * lo_cos[...] - hi_sin[:, a : a + 1] * lo_sin[...]
        out[:, a * width : a * width + size] = block[:, :size].astype(out.dtype)
    height = lo_cos_t.shape[0]
    for a in range(hi_cos_t.shape[0]):
        block = hi_cos_t[a : a + 1, :] * lo_cos_t[...] - hi_sin_t[a : a + 1, :] * lo_sin_t[...]
        out_t[a * height : (a + 1) * height, :] = block.astype(out_t.dtype)


def fourier_tables(wave_of_slot, sources, longitudes):
    per_source = wave_of_slot.shape[0] // sources
    waves = (wave_of_slot + 1).reshape(sources, per_source).T
    waves = jnp.stack([waves, waves], axis=1).reshape(-1)
    terms = waves.shape[0]
    cosine = jnp.arange(terms, dtype=jnp.int32) // sources % 2
    quarter = cosine * (longitudes // 4)
    none = jnp.zeros_like(quarter)
    width = 128
    height = 16 * math.gcd(longitudes // 16, 10)
    wide = angle_parts(waves, width, -(-longitudes // width), quarter, longitudes, 1)
    wide += angle_parts(waves, 1, width, none, longitudes, 1)
    tall = angle_parts(waves, height, longitudes // height, quarter, longitudes, 0)
    tall += angle_parts(waves, 1, height, none, longitudes, 0)
    return pl.pallas_call(
        table_kernel,
        out_shape=(
            jax.ShapeDtypeStruct((terms, longitudes), jnp.bfloat16),
            jax.ShapeDtypeStruct((longitudes, terms), jnp.bfloat16),
        ),
        compiler_params=pltpu.CompilerParams(vmem_limit_bytes=VMEM_BYTES),
        cost_estimate=pl.CostEstimate(
            flops=6 * terms * longitudes, bytes_accessed=4 * terms * longitudes, transcendentals=0
        ),
        name="fourier_tables",
    )(*wide, *tall)


def silu(v):
    half = 0.5 * v
    return half + half * jnp.tanh(half)


def columns_kernel(
    sources,
    weight_ref,
    rows_ref,
    table_ref,
    table_t_ref,
    surface_ref,
    first_ref,
    first_bias_ref,
    mid_ref,
    mid_bias_ref,
    last_ref,
    out_ref,
    wide_in,
    wide_out,
    coefficients,
    tendency,
):
    step = pl.program_id(0)
    features = rows_ref.shape[1]
    longitudes = table_ref.shape[1]
    terms = table_ref.shape[0] // sources
    stride = rows_ref.shape[0] // sources
    group = surface_ref.shape[0] // longitudes

    @pl.when(step == 0)
    def _():
        wide_in[...] = rows_ref[...].astype(jnp.float32)

    for j in range(group):
        lat = step * group + j
        for q in range(terms):
            coefficients[q * sources : (q + 1) * sources, j * features : (j + 1) * features] = (
                wide_in[pl.ds(terms * lat + q, sources, stride), :].astype(jnp.bfloat16)
            )

    tile = longitudes // 3
    for start in range(0, longitudes, tile):
        grid_state = jnp.dot(
            table_t_ref[start : start + tile, :],
            coefficients[...],
            preferred_element_type=jnp.float32,
        ).astype(jnp.bfloat16)
        for j in range(group):
            at = j * longitudes + start
            joined = jnp.concatenate(
                [grid_state[:, j * features : (j + 1) * features], surface_ref[at : at + tile, :]],
                axis=1,
            )
            first = jnp.dot(joined, first_ref[...], preferred_element_type=jnp.float32)
            first = silu(first + first_bias_ref[...]).astype(jnp.bfloat16)
            second = jnp.dot(first, mid_ref[...], preferred_element_type=jnp.float32)
            second = silu(second + mid_bias_ref[...]).astype(jnp.bfloat16)
            tendency[start : start + tile, j * features : (j + 1) * features] = jnp.dot(
                second, last_ref[...], preferred_element_type=jnp.float32
            ).astype(jnp.bfloat16)

    spectrum = jnp.dot(table_ref[...], tendency[...], preferred_element_type=jnp.float32)
    for j in range(group):
        lat = step * group + j
        scaled = spectrum[:, j * features : (j + 1) * features] * weight_ref[lat]
        for q in range(terms):
            wide_out[pl.ds(terms * lat + q, sources, stride), :] = scaled[
                q * sources : (q + 1) * sources, :
            ]

    @pl.when(step == pl.num_programs(0) - 1)
    def _():
        out_ref[...] = wide_out[...].astype(out_ref.dtype)


def column_spectrum(
    rows, tables, surface_rows, quad_weight, sources, first, first_bias, mid, mid_bias, last
):
    table, table_t = tables
    terms, longitudes = table.shape
    features = rows.shape[1]
    lats = quad_weight.shape[0]
    group = 2 if lats % 2 == 0 else 1
    hidden = first.shape[1]
    columns = lats * longitudes
    flops = 2 * columns * (2 * terms * features + 2 * features * hidden)
    flops += 2 * columns * (hidden * hidden + hidden * features)
    return pl.pallas_call(
        functools.partial(columns_kernel, sources),
        grid=(lats // group,),
        in_specs=[
            pl.BlockSpec(memory_space=pltpu.SMEM),
            whole(rows.shape),
            whole(table.shape),
            whole(table_t.shape),
            pl.BlockSpec((group * longitudes, surface_rows.shape[1]), lambda i: (i, 0)),
            whole(first.shape),
            whole((1, hidden)),
            whole(mid.shape),
            whole((1, hidden)),
            whole(last.shape),
        ],
        out_specs=whole(rows.shape),
        out_shape=jax.ShapeDtypeStruct(rows.shape, jnp.bfloat16),
        scratch_shapes=[
            pltpu.VMEM(rows.shape, jnp.float32),
            pltpu.VMEM(rows.shape, jnp.float32),
            pltpu.VMEM((terms, group * features), jnp.bfloat16),
            pltpu.VMEM((longitudes, group * features), jnp.bfloat16),
        ],
        compiler_params=pltpu.CompilerParams(vmem_limit_bytes=VMEM_BYTES),
        cost_estimate=pl.CostEstimate(
            flops=flops,
            bytes_accessed=2 * (2 * rows.size + 2 * table.size + surface_rows.size),
            transcendentals=2 * columns * hidden,
        ),
        name="column_spectrum",
    )(
        quad_weight,
        rows,
        table,
        table_t,
        surface_rows,
        first,
        first_bias.reshape(1, hidden),
        mid,
        mid_bias.reshape(1, hidden),
        last,
    )


def exchange(chunks):
    return lax.all_to_all(chunks, "band", split_axis=0, concat_axis=0, tiled=True)


def surface_of_columns(dest_owner, dest_slot, surface):
    owners = lax.axis_size("band")
    members = lax.axis_size("ens")
    held, features = surface.shape
    total = dest_owner.size
    per_owner = total // owners
    quota = -(-per_owner // members)
    padded = -(-quota // 16) * 16
    columns = jnp.arange(total, dtype=jnp.int32)
    keys = (dest_owner * held + dest_slot).reshape(-1)
    keys, order = lax.sort((keys, columns), num_keys=1)
    slots = keys.reshape(owners, per_owner) - jnp.arange(owners, dtype=jnp.int32)[:, None] * held
    slots = jnp.pad(slots, ((0, 0), (0, quota * members - per_owner)))
    mine = lax.dynamic_slice_in_dim(slots, lax.axis_index("ens") * quota, quota, axis=1)
    wanted = exchange(mine.reshape(owners, 1, quota)).reshape(owners, quota)
    wanted = jnp.pad(wanted, ((0, 0), (0, padded - quota)))
    replies = surface.at[wanted.reshape(-1)].get(mode="promise_in_bounds")
    fetched = exchange(replies.reshape(owners, padded, features))
    everything = lax.all_gather(fetched.reshape(-1, features), "ens", axis=0, tiled=True)
    _, places = lax.sort((order, columns), num_keys=1)
    owner, rank = places // per_owner, places % per_owner
    source = ((rank // quota) * owners + owner) * padded + rank % quota
    return everything.at[source].get(mode="promise_in_bounds")


def local(
    spectral_state,
    lat_basis,
    quad_weight,
    wave_of_slot,
    dest_owner,
    dest_slot,
    surface,
    in_weight,
    surface_weight,
    in_bias,
    mid_weight,
    mid_bias,
    out_weight,
):
    bands = lax.axis_size("band")
    longitudes = dest_owner.shape[1]
    surface_rows = surface_of_columns(dest_owner, dest_slot, surface)
    fourier = to_latitudes(lat_basis, spectral_state)
    features = fourier.shape[1]
    banded = exchange(fourier.reshape(bands, -1, features)).reshape(-1, features)
    tables = fourier_tables(wave_of_slot, bands, longitudes)
    spectrum = column_spectrum(
        banded,
        tables,
        surface_rows,
        quad_weight * math.sqrt(2.0 / longitudes),
        bands,
        jnp.concatenate([in_weight, surface_weight], axis=0),
        in_bias,
        mid_weight,
        mid_bias,
        out_weight,
    )
    owned = exchange(spectrum.reshape(bands, -1, features)).reshape(-1, features)
    return to_degrees(lat_basis, owned)


def solution(mesh):
    return jax.shard_map(
        local,
        mesh=mesh,
        in_specs=(
            P(("ens", "band"), None, None),
            P("band", None, None),
            P("band"),
            P(),
            P("band", None),
            P("band", None),
            P("band", None),
            P(),
            P(),
            P(),
            P(),
            P(),
            P(),
        ),
        out_specs=P(("ens", "band"), None, None),
        check_vma=False,
    )
```

```python
import functools
import math

import jax
import jax.numpy as jnp
from jax import lax
from jax.experimental import pallas as pl
from jax.experimental.pallas import tpu as pltpu
from jax.sharding import PartitionSpec as P

VMEM_BYTES = 48 * 1024 * 1024


def whole(shape):
    zeros = (0,) * len(shape)
    return pl.BlockSpec(shape, lambda *_: zeros)


def fourier_kernel(basis_ref, state_ref, out_ref, wide):
    slots, lats, features = pl.num_programs(0), basis_ref.shape[1], out_ref.shape[1]
    slot = pl.program_id(0)
    per_lat = out_ref.shape[0] // lats
    found = jnp.dot(basis_ref[0], state_ref[0], preferred_element_type=jnp.float32)
    for k in range(2):
        wide[pl.ds(2 * slot + k, lats, per_lat), :] = found[:, k * features : (k + 1) * features]

    @pl.when(slot == slots - 1)
    def _():
        out_ref[...] = wide[...].astype(out_ref.dtype)


def to_latitudes(lat_basis, spectral_state):
    slots, lats, degrees = lat_basis.shape
    features = spectral_state.shape[2] // 2
    rows = lats * slots * 2
    return pl.pallas_call(
        fourier_kernel,
        grid=(slots,),
        in_specs=[
            pl.BlockSpec((1, lats, degrees), lambda s: (s, 0, 0)),
            pl.BlockSpec((1, degrees, 2 * features), lambda s: (s, 0, 0)),
        ],
        out_specs=whole((rows, features)),
        out_shape=jax.ShapeDtypeStruct((rows, features), jnp.bfloat16),
        scratch_shapes=[pltpu.VMEM((rows, features), jnp.float32)],
        compiler_params=pltpu.CompilerParams(vmem_limit_bytes=VMEM_BYTES),
        cost_estimate=pl.CostEstimate(
            flops=2 * slots * lats * degrees * 2 * features,
            bytes_accessed=2 * (lat_basis.size + spectral_state.size + rows * features),
            transcendentals=0,
        ),
        name="to_latitudes",
    )(lat_basis, spectral_state)


def degrees_kernel(basis_ref, rows_ref, out_ref, wide):
    lats = basis_ref.shape[1]
    slot = pl.program_id(0)
    per_lat = rows_ref.shape[0] // lats

    @pl.when(slot == 0)
    def _():
        wide[...] = rows_ref[...].astype(jnp.float32)

    spectrum = jnp.concatenate(
        [wide[pl.ds(2 * slot + k, lats, per_lat), :].astype(jnp.bfloat16) for k in range(2)],
        axis=1,
    )
    out_ref[0] = lax.dot_general(
        basis_ref[0], spectrum, (((0,), (0,)), ((), ())), preferred_element_type=jnp.float32
    )


def to_degrees(lat_basis, rows):
    slots, lats, degrees = lat_basis.shape
    features = rows.shape[1]
    return pl.pallas_call(
        degrees_kernel,
        grid=(slots,),
        in_specs=[
            pl.BlockSpec((1, lats, degrees), lambda s: (s, 0, 0)),
            whole(rows.shape),
        ],
        out_specs=pl.BlockSpec((1, degrees, 2 * features), lambda s: (s, 0, 0)),
        out_shape=jax.ShapeDtypeStruct((slots, degrees, 2 * features), jnp.float32),
        scratch_shapes=[pltpu.VMEM(rows.shape, jnp.float32)],
        compiler_params=pltpu.CompilerParams(vmem_limit_bytes=VMEM_BYTES),
        cost_estimate=pl.CostEstimate(
            flops=2 * slots * lats * degrees * 2 * features,
            bytes_accessed=2 * (lat_basis.size + rows.size) + 8 * slots * degrees * features,
            transcendentals=0,
        ),
        name="to_degrees",
    )(lat_basis, rows)


def angle_parts(waves, step, count, quarter, longitudes, axis):
    positions = jnp.arange(count, dtype=jnp.int32) * step
    shape = (-1, 1) if axis == 1 else (1, -1)
    phases = waves.reshape(shape) * positions.reshape(shape[::-1])
    phases = (phases + quarter.reshape(shape)) % longitudes
    angles = phases.astype(jnp.float32) * (2.0 * math.pi / longitudes)
    return jnp.cos(angles), jnp.sin(angles)


def table_kernel(hi_cos, hi_sin, lo_cos, lo_sin, hi_cos_t, hi_sin_t, lo_cos_t, lo_sin_t, out, out_t):
    longitudes = out.shape[1]
    width = lo_cos.shape[1]
    for a in range(hi_cos.shape[1]):
        size = min(width, longitudes - a * width)
        block = hi_cos[:, a : a + 1] * lo_cos[...] - hi_sin[:, a : a + 1] * lo_sin[...]
        out[:, a * width : a * width + size] = block[:, :size].astype(out.dtype)
    height = lo_cos_t.shape[0]
    for a in range(hi_cos_t.shape[0]):
        block = hi_cos_t[a : a + 1, :] * lo_cos_t[...] - hi_sin_t[a : a + 1, :] * lo_sin_t[...]
        out_t[a * height : (a + 1) * height, :] = block.astype(out_t.dtype)


def fourier_tables(wave_of_slot, sources, longitudes):
    per_source = wave_of_slot.shape[0] // sources
    waves = (wave_of_slot + 1).reshape(sources, per_source).T
    waves = jnp.stack([waves, waves], axis=1).reshape(-1)
    terms = waves.shape[0]
    cosine = jnp.arange(terms, dtype=jnp.int32) // sources % 2
    quarter = cosine * (longitudes // 4)
    none = jnp.zeros_like(quarter)
    width = 128
    height = 16 * math.gcd(longitudes // 16, 10)
    wide = angle_parts(waves, width, -(-longitudes // width), quarter, longitudes, 1)
    wide += angle_parts(waves, 1, width, none, longitudes, 1)
    tall = angle_parts(waves, height, longitudes // height, quarter, longitudes, 0)
    tall += angle_parts(waves, 1, height, none, longitudes, 0)
    return pl.pallas_call(
        table_kernel,
        out_shape=(
            jax.ShapeDtypeStruct((terms, longitudes), jnp.bfloat16),
            jax.ShapeDtypeStruct((longitudes, terms), jnp.bfloat16),
        ),
        compiler_params=pltpu.CompilerParams(vmem_limit_bytes=VMEM_BYTES),
        cost_estimate=pl.CostEstimate(
            flops=6 * terms * longitudes, bytes_accessed=4 * terms * longitudes, transcendentals=0
        ),
        name="fourier_tables",
    )(*wide, *tall)


def silu(v):
    half = 0.5 * v
    return half + half * jnp.tanh(half)


def columns_kernel(
    sources,
    weight_ref,
    rows_ref,
    table_ref,
    table_t_ref,
    surface_ref,
    first_ref,
    first_bias_ref,
    mid_ref,
    mid_bias_ref,
    last_ref,
    out_ref,
    wide_in,
    wide_out,
    coefficients,
    tendency,
):
    step = pl.program_id(0)
    features = rows_ref.shape[1]
    longitudes = table_ref.shape[1]
    terms = table_ref.shape[0] // sources
    stride = rows_ref.shape[0] // sources
    group = surface_ref.shape[0] // longitudes

    @pl.when(step == 0)
    def _():
        wide_in[...] = rows_ref[...].astype(jnp.float32)

    for j in range(group):
        lat = step * group + j
        for q in range(terms):
            coefficients[q * sources : (q + 1) * sources, j * features : (j + 1) * features] = (
                wide_in[pl.ds(terms * lat + q, sources, stride), :].astype(jnp.bfloat16)
            )

    tile = longitudes // 3
    for start in range(0, longitudes, tile):
        grid_state = jnp.dot(
            table_t_ref[start : start + tile, :],
            coefficients[...],
            preferred_element_type=jnp.float32,
        ).astype(jnp.bfloat16)
        for j in range(group):
            at = j * longitudes + start
            joined = jnp.concatenate(
                [grid_state[:, j * features : (j + 1) * features], surface_ref[at : at + tile, :]],
                axis=1,
            )
            first = jnp.dot(joined, first_ref[...], preferred_element_type=jnp.float32)
            first = silu(first + first_bias_ref[...]).astype(jnp.bfloat16)
            second = jnp.dot(first, mid_ref[...], preferred_element_type=jnp.float32)
            second = silu(second + mid_bias_ref[...]).astype(jnp.bfloat16)
            tendency[start : start + tile, j * features : (j + 1) * features] = jnp.dot(
                second, last_ref[...], preferred_element_type=jnp.float32
            ).astype(jnp.bfloat16)

    spectrum = jnp.dot(table_ref[...], tendency[...], preferred_element_type=jnp.float32)
    for j in range(group):
        lat = step * group + j
        scaled = spectrum[:, j * features : (j + 1) * features] * weight_ref[lat]
        for q in range(terms):
            wide_out[pl.ds(terms * lat + q, sources, stride), :] = scaled[
                q * sources : (q + 1) * sources, :
            ]

    @pl.when(step == pl.num_programs(0) - 1)
    def _():
        out_ref[...] = wide_out[...].astype(out_ref.dtype)


def column_spectrum(
    rows, tables, surface_rows, quad_weight, sources, first, first_bias, mid, mid_bias, last
):
    table, table_t = tables
    terms, longitudes = table.shape
    features = rows.shape[1]
    lats = quad_weight.shape[0]
    group = 2 if lats % 2 == 0 else 1
    hidden = first.shape[1]
    columns = lats * longitudes
    flops = 2 * columns * (2 * terms * features + 2 * features * hidden)
    flops += 2 * columns * (hidden * hidden + hidden * features)
    return pl.pallas_call(
        functools.partial(columns_kernel, sources),
        grid=(lats // group,),
        in_specs=[
            pl.BlockSpec(memory_space=pltpu.SMEM),
            whole(rows.shape),
            whole(table.shape),
            whole(table_t.shape),
            pl.BlockSpec((group * longitudes, surface_rows.shape[1]), lambda i: (i, 0)),
            whole(first.shape),
            whole((1, hidden)),
            whole(mid.shape),
            whole((1, hidden)),
            whole(last.shape),
        ],
        out_specs=whole(rows.shape),
        out_shape=jax.ShapeDtypeStruct(rows.shape, jnp.bfloat16),
        scratch_shapes=[
            pltpu.VMEM(rows.shape, jnp.float32),
            pltpu.VMEM(rows.shape, jnp.float32),
            pltpu.VMEM((terms, group * features), jnp.bfloat16),
            pltpu.VMEM((longitudes, group * features), jnp.bfloat16),
        ],
        compiler_params=pltpu.CompilerParams(vmem_limit_bytes=VMEM_BYTES),
        cost_estimate=pl.CostEstimate(
            flops=flops,
            bytes_accessed=2 * (2 * rows.size + 2 * table.size + surface_rows.size),
            transcendentals=2 * columns * hidden,
        ),
        name="column_spectrum",
    )(
        quad_weight,
        rows,
        table,
        table_t,
        surface_rows,
        first,
        first_bias.reshape(1, hidden),
        mid,
        mid_bias.reshape(1, hidden),
        last,
    )


def exchange(chunks):
    return lax.all_to_all(chunks, "band", split_axis=0, concat_axis=0, tiled=True)


def fetch_kernel(ids_ref, held_ref, out_ref, wide, found):
    wide[...] = held_ref[...].astype(jnp.float32)
    count = ids_ref.shape[2]

    def one_peer(peer, carry):
        base = pl.multiple_of(peer * count, count)
        for i in range(count):
            found[pl.ds(base + i, 1), :] = wide[pl.ds(ids_ref[peer, 0, i], 1), :]
        return carry

    lax.fori_loop(0, ids_ref.shape[0], one_peer, 0)
    out_ref[...] = found[...].astype(out_ref.dtype)


def fetch_rows(ids, held):
    rows = ids.shape[0] * ids.shape[2]
    features = held.shape[1]
    return pl.pallas_call(
        fetch_kernel,
        in_specs=[pl.BlockSpec(memory_space=pltpu.SMEM), pl.BlockSpec(memory_space=pltpu.VMEM)],
        out_specs=pl.BlockSpec(memory_space=pltpu.VMEM),
        out_shape=jax.ShapeDtypeStruct((rows, features), held.dtype),
        scratch_shapes=[
            pltpu.VMEM(held.shape, jnp.float32),
            pltpu.VMEM((rows, features), jnp.float32),
        ],
        compiler_params=pltpu.CompilerParams(vmem_limit_bytes=VMEM_BYTES),
        cost_estimate=pl.CostEstimate(
            flops=0, bytes_accessed=20 * 2 * (held.size + rows * features), transcendentals=0
        ),
        name="fetch_rows",
    )(ids, held)


def arrange_kernel(unroll, places_ref, *refs):
    pieces, out_ref, wide, found = refs[:-3], refs[-3], refs[-2], refs[-1]
    step = pl.program_id(0)
    rows = out_ref.shape[0]

    @pl.when(step == 0)
    def _():
        at = 0
        for piece in pieces:
            wide[at : at + piece.shape[0], :] = piece[...].astype(jnp.float32)
            at += piece.shape[0]

    def one_block(block, carry):
        base = pl.multiple_of(block * unroll, unroll)
        for i in range(unroll):
            found[pl.ds(base + i, 1), :] = wide[pl.ds(places_ref[step * rows + base + i], 1), :]
        return carry

    lax.fori_loop(0, rows // unroll, one_block, 0)
    out_ref[...] = found[...].astype(out_ref.dtype)


def arrange_rows(places, pieces):
    total = places.shape[0]
    features = pieces[0].shape[1]
    steps, unroll = 5, 96
    rows = total // steps
    received = sum(piece.shape[0] for piece in pieces)
    return pl.pallas_call(
        functools.partial(arrange_kernel, unroll),
        grid=(steps,),
        in_specs=[pl.BlockSpec(memory_space=pltpu.SMEM)] + [whole(p.shape) for p in pieces],
        out_specs=pl.BlockSpec((rows, features), lambda i: (i, 0)),
        out_shape=jax.ShapeDtypeStruct((total, features), jnp.bfloat16),
        scratch_shapes=[
            pltpu.VMEM((received, features), jnp.float32),
            pltpu.VMEM((rows, features), jnp.float32),
        ],
        compiler_params=pltpu.CompilerParams(vmem_limit_bytes=VMEM_BYTES),
        cost_estimate=pl.CostEstimate(
            flops=0, bytes_accessed=15 * 2 * (total + received) * features // 4, transcendentals=0
        ),
        name="arrange_rows",
    )(places, *pieces)


def around_members(piece):
    members = lax.axis_size("ens")
    up = [(i, (i + 1) % members) for i in range(members)]
    down = [(i, (i - 1) % members) for i in range(members)]
    half = piece.shape[0] // 2
    below = lax.ppermute(piece, "ens", up)
    above = lax.ppermute(piece, "ens", down)
    far_first = lax.ppermute(below[:half], "ens", up)
    far_second = lax.ppermute(above[half:], "ens", down)
    return piece, above, far_first, far_second, below


def requests(dest_owner, dest_slot, held):
    owners = lax.axis_size("band")
    members = lax.axis_size("ens")
    total = dest_owner.size
    per_owner = total // owners
    quota = -(-per_owner // members)
    padded = -(-quota // 16) * 16
    columns = jnp.arange(total, dtype=jnp.int32)
    keys = (dest_owner * held + dest_slot).reshape(-1)
    keys, order = lax.sort((keys, columns), num_keys=1)
    slots = keys.reshape(owners, per_owner) - jnp.arange(owners, dtype=jnp.int32)[:, None] * held
    slots = jnp.pad(slots, ((0, 0), (0, quota * members - per_owner)))
    mine = lax.dynamic_slice_in_dim(slots, lax.axis_index("ens") * quota, quota, axis=1)
    mine = jnp.pad(mine, ((0, 0), (0, padded - quota)))
    return mine.reshape(owners, 1, padded), order


def places_of_columns(order, quota, padded):
    owners = lax.axis_size("band")
    members = lax.axis_size("ens")
    total = order.shape[0]
    per_owner = total // owners
    _, places = lax.sort((order, jnp.arange(total, dtype=jnp.int32)), num_keys=1)
    owner, rank = places // per_owner, places % per_owner
    away = (rank // quota - lax.axis_index("ens")) % members
    return (away * owners + owner) * padded + rank % quota


def local(
    spectral_state,
    lat_basis,
    quad_weight,
    wave_of_slot,
    dest_owner,
    dest_slot,
    surface,
    in_weight,
    surface_weight,
    in_bias,
    mid_weight,
    mid_bias,
    out_weight,
):
    bands = lax.axis_size("band")
    longitudes = dest_owner.shape[1]
    ids, order = requests(dest_owner, dest_slot, surface.shape[0])
    padded = ids.shape[2]
    quota = -(-(order.shape[0] // bands) // lax.axis_size("ens"))
    replies = fetch_rows(exchange(ids), surface)
    fourier = to_latitudes(lat_basis, spectral_state)
    replies, fourier = lax.optimization_barrier((replies, fourier))
    features = fourier.shape[1]
    fetched = exchange(replies.reshape(bands, padded, -1)).reshape(-1, surface.shape[1])
    places = places_of_columns(order, quota, padded)
    surface_rows = arrange_rows(places, around_members(fetched))
    banded = exchange(fourier.reshape(bands, -1, features)).reshape(-1, features)
    tables = fourier_tables(wave_of_slot, bands, longitudes)
    spectrum = column_spectrum(
        banded,
        tables,
        surface_rows,
        quad_weight * math.sqrt(2.0 / longitudes),
        bands,
        jnp.concatenate([in_weight, surface_weight], axis=0),
        in_bias,
        mid_weight,
        mid_bias,
        out_weight,
    )
    owned = exchange(spectrum.reshape(bands, -1, features)).reshape(-1, features)
    return to_degrees(lat_basis, owned)


def solution(mesh):
    return jax.shard_map(
        local,
        mesh=mesh,
        in_specs=(
            P(("ens", "band"), None, None),
            P("band", None, None),
            P("band"),
            P(),
            P("band", None),
            P("band", None),
            P("band", None),
            P(),
            P(),
            P(),
            P(),
            P(),
            P(),
        ),
        out_specs=P(("ens", "band"), None, None),
        check_vma=False,
    )
```

```python
import functools
import math

import jax
import jax.numpy as jnp
from jax import lax
from jax.experimental import pallas as pl
from jax.experimental.pallas import tpu as pltpu
from jax.sharding import PartitionSpec as P

VMEM_BYTES = 24 * 1024 * 1024


def whole(shape):
    zeros = (0,) * len(shape)
    return pl.BlockSpec(shape, lambda *_: zeros)


def fourier_kernel(basis_ref, state_ref, out_ref, wide):
    slots, lats, features = pl.num_programs(0), basis_ref.shape[1], out_ref.shape[1]
    slot = pl.program_id(0)
    per_lat = out_ref.shape[0] // lats
    found = jnp.dot(basis_ref[0], state_ref[0], preferred_element_type=jnp.float32)
    for k in range(2):
        wide[pl.ds(2 * slot + k, lats, per_lat), :] = found[:, k * features : (k + 1) * features]

    @pl.when(slot == slots - 1)
    def _():
        out_ref[...] = wide[...].astype(out_ref.dtype)


def to_latitudes(lat_basis, spectral_state):
    slots, lats, degrees = lat_basis.shape
    features = spectral_state.shape[2] // 2
    rows = lats * slots * 2
    return pl.pallas_call(
        fourier_kernel,
        grid=(slots,),
        in_specs=[
            pl.BlockSpec((1, lats, degrees), lambda s: (s, 0, 0)),
            pl.BlockSpec((1, degrees, 2 * features), lambda s: (s, 0, 0)),
        ],
        out_specs=whole((rows, features)),
        out_shape=jax.ShapeDtypeStruct((rows, features), jnp.bfloat16),
        scratch_shapes=[pltpu.VMEM((rows, features), jnp.float32)],
        compiler_params=pltpu.CompilerParams(vmem_limit_bytes=VMEM_BYTES),
        cost_estimate=pl.CostEstimate(
            flops=2 * slots * lats * degrees * 2 * features,
            bytes_accessed=2 * (lat_basis.size + spectral_state.size + rows * features),
            transcendentals=0,
        ),
        name="to_latitudes",
    )(lat_basis, spectral_state)


def degrees_kernel(basis_ref, rows_ref, out_ref, wide):
    lats = basis_ref.shape[1]
    slot = pl.program_id(0)
    per_lat = rows_ref.shape[0] // lats

    @pl.when(slot == 0)
    def _():
        wide[...] = rows_ref[...].astype(jnp.float32)

    spectrum = jnp.concatenate(
        [wide[pl.ds(2 * slot + k, lats, per_lat), :].astype(jnp.bfloat16) for k in range(2)],
        axis=1,
    )
    out_ref[0] = lax.dot_general(
        basis_ref[0], spectrum, (((0,), (0,)), ((), ())), preferred_element_type=jnp.float32
    )


def to_degrees(lat_basis, rows):
    slots, lats, degrees = lat_basis.shape
    features = rows.shape[1]
    return pl.pallas_call(
        degrees_kernel,
        grid=(slots,),
        in_specs=[
            pl.BlockSpec((1, lats, degrees), lambda s: (s, 0, 0)),
            whole(rows.shape),
        ],
        out_specs=pl.BlockSpec((1, degrees, 2 * features), lambda s: (s, 0, 0)),
        out_shape=jax.ShapeDtypeStruct((slots, degrees, 2 * features), jnp.float32),
        scratch_shapes=[pltpu.VMEM(rows.shape, jnp.float32)],
        compiler_params=pltpu.CompilerParams(vmem_limit_bytes=VMEM_BYTES),
        cost_estimate=pl.CostEstimate(
            flops=2 * slots * lats * degrees * 2 * features,
            bytes_accessed=2 * (lat_basis.size + rows.size) + 8 * slots * degrees * features,
            transcendentals=0,
        ),
        name="to_degrees",
    )(lat_basis, rows)


def angle_parts(waves, step, count, quarter, longitudes, axis):
    positions = jnp.arange(count, dtype=jnp.int32) * step
    shape = (-1, 1) if axis == 1 else (1, -1)
    phases = waves.reshape(shape) * positions.reshape(shape[::-1])
    phases = (phases + quarter.reshape(shape)) % longitudes
    angles = phases.astype(jnp.float32) * (2.0 * math.pi / longitudes)
    return jnp.cos(angles), jnp.sin(angles)


def table_kernel(hi_cos, hi_sin, lo_cos, lo_sin, hi_cos_t, hi_sin_t, lo_cos_t, lo_sin_t, out, out_t):
    longitudes = out.shape[1]
    width = lo_cos.shape[1]
    for a in range(hi_cos.shape[1]):
        size = min(width, longitudes - a * width)
        block = hi_cos[:, a : a + 1] * lo_cos[...] - hi_sin[:, a : a + 1] * lo_sin[...]
        out[:, a * width : a * width + size] = block[:, :size].astype(out.dtype)
    height = lo_cos_t.shape[0]
    for a in range(hi_cos_t.shape[0]):
        block = hi_cos_t[a : a + 1, :] * lo_cos_t[...] - hi_sin_t[a : a + 1, :] * lo_sin_t[...]
        out_t[a * height : (a + 1) * height, :] = block.astype(out_t.dtype)


def fourier_tables(wave_of_slot, sources, longitudes):
    per_source = wave_of_slot.shape[0] // sources
    waves = (wave_of_slot + 1).reshape(sources, per_source).T.reshape(-1)
    waves = jnp.concatenate([waves, waves])
    terms = waves.shape[0]
    quarter = jnp.arange(terms, dtype=jnp.int32) // (terms // 2) * (longitudes // 4)
    none = jnp.zeros_like(quarter)
    width, height = 128, 32
    kept = -(-(longitudes // 2 + 1) // height) * height
    wide = angle_parts(waves, width, -(-kept // width), quarter, longitudes, 1)
    wide += angle_parts(waves, 1, width, none, longitudes, 1)
    tall = angle_parts(waves, height, kept // height, quarter, longitudes, 0)
    tall += angle_parts(waves, 1, height, none, longitudes, 0)
    return pl.pallas_call(
        table_kernel,
        out_shape=(
            jax.ShapeDtypeStruct((terms, kept), jnp.bfloat16),
            jax.ShapeDtypeStruct((kept, terms), jnp.bfloat16),
        ),
        compiler_params=pltpu.CompilerParams(vmem_limit_bytes=VMEM_BYTES),
        cost_estimate=pl.CostEstimate(
            flops=6 * terms * kept, bytes_accessed=4 * terms * kept, transcendentals=0
        ),
        name="fourier_tables",
    )(*wide, *tall)


def silu(v):
    half = 0.5 * v
    return half + half * jnp.tanh(half)


def columns_kernel(
    sources,
    weight_ref,
    rows_ref,
    table_ref,
    table_t_ref,
    surface_ref,
    first_ref,
    first_bias_ref,
    mid_ref,
    mid_bias_ref,
    last_ref,
    out_ref,
    wide_in,
    wide_out,
    coefficients,
    evens,
    odds,
):
    step = pl.program_id(0)
    features = rows_ref.shape[1]
    terms = table_ref.shape[0] // sources
    kept = table_ref.shape[1]
    stride = rows_ref.shape[0] // sources
    lanes = coefficients.shape[1]
    group = lanes // features
    half = surface_ref.shape[0] // group // 2
    split = table_ref.shape[0] // 2

    @pl.when(step == 0)
    def _():
        wide_in[...] = rows_ref[...].astype(jnp.float32)

    def place_of(q):
        return (q % 2) * split + q // 2 * sources

    for j in range(group):
        lat = step * group + j
        for q in range(terms):
            at = place_of(q)
            coefficients[at : at + sources, j * features : (j + 1) * features] = wide_in[
                pl.ds(terms * lat + q, sources, stride), :
            ].astype(jnp.bfloat16)

    def network(state, start):
        joined = jnp.concatenate(
            [
                jnp.concatenate(
                    [
                        state[:, j * features : (j + 1) * features].astype(jnp.bfloat16),
                        surface_ref[2 * half * j + start : 2 * half * j + start + tile, :],
                    ],
                    axis=1,
                )
                for j in range(group)
            ],
            axis=0,
        )
        first = jnp.dot(joined, first_ref[...], preferred_element_type=jnp.float32)
        first = silu(first + first_bias_ref[...]).astype(jnp.bfloat16)
        second = jnp.dot(first, mid_ref[...], preferred_element_type=jnp.float32)
        second = silu(second + mid_bias_ref[...]).astype(jnp.bfloat16)
        third = jnp.dot(second, last_ref[...], preferred_element_type=jnp.float32)
        return jnp.concatenate([third[j * tile : (j + 1) * tile, :] for j in range(group)], axis=1)

    tile = half // 3
    lone = None
    for start in (2 * tile, tile, 0):
        end = kept if lone is None else start + tile
        even = jnp.dot(
            table_t_ref[start:end, :split],
            coefficients[:split, :],
            preferred_element_type=jnp.float32,
        )
        odd = jnp.dot(
            table_t_ref[start : start + tile, split:],
            coefficients[split:, :],
            preferred_element_type=jnp.float32,
        )
        if lone is None:
            lone = even[tile : tile + 1, :]
            even = even[:tile, :]
        east, west = even + odd, even - odd
        top = lax.broadcasted_iota(jnp.int32, (tile, lanes), 0) == 0
        if start == 0:
            west = jnp.where(top, lone, west)
        east, west = network(east, start), network(west, half + start)
        if start == 0:
            evens[:tile, :] = jnp.where(top, east, east + west).astype(jnp.bfloat16)
            evens[half:, :] = jnp.where(top[: kept - half, :], west[: kept - half, :], 0.0).astype(
                jnp.bfloat16
            )
            odds[half:, :] = jnp.zeros((kept - half, lanes), jnp.bfloat16)
        else:
            evens[start : start + tile, :] = (east + west).astype(jnp.bfloat16)
        odds[start : start + tile, :] = (east - west).astype(jnp.bfloat16)

    for k, halves in enumerate((evens, odds)):
        spectrum = jnp.dot(
            table_ref[k * split : (k + 1) * split, :],
            halves[...],
            preferred_element_type=jnp.float32,
        )
        for j in range(group):
            lat = step * group + j
            scaled = spectrum[:, j * features : (j + 1) * features] * weight_ref[lat]
            for q in range(k, terms, 2):
                at = q // 2 * sources
                wide_out[pl.ds(terms * lat + q, sources, stride), :] = scaled[at : at + sources, :]

    @pl.when(step == pl.num_programs(0) - 1)
    def _():
        out_ref[...] = wide_out[...].astype(out_ref.dtype)


def column_spectrum(
    rows, tables, surface_rows, quad_weight, sources, first, first_bias, mid, mid_bias, last
):
    table, table_t = tables
    terms, kept = table.shape
    longitudes = surface_rows.shape[0] // quad_weight.shape[0]
    features = rows.shape[1]
    lats = quad_weight.shape[0]
    group = 2 if lats % 2 == 0 else 1
    hidden = first.shape[1]
    columns = lats * longitudes
    flops = 2 * columns * (terms * features + 2 * features * hidden)
    flops += 2 * columns * (hidden * hidden + hidden * features)
    return pl.pallas_call(
        functools.partial(columns_kernel, sources),
        grid=(lats // group,),
        in_specs=[
            pl.BlockSpec(memory_space=pltpu.SMEM),
            whole(rows.shape),
            whole(table.shape),
            whole(table_t.shape),
            pl.BlockSpec((group * longitudes, surface_rows.shape[1]), lambda i: (i, 0)),
            whole(first.shape),
            whole((1, hidden)),
            whole(mid.shape),
            whole((1, hidden)),
            whole(last.shape),
        ],
        out_specs=whole(rows.shape),
        out_shape=jax.ShapeDtypeStruct(rows.shape, jnp.bfloat16),
        scratch_shapes=[
            pltpu.VMEM(rows.shape, jnp.float32),
            pltpu.VMEM(rows.shape, jnp.float32),
            pltpu.VMEM((terms, group * features), jnp.bfloat16),
            pltpu.VMEM((kept, group * features), jnp.bfloat16),
            pltpu.VMEM((kept, group * features), jnp.bfloat16),
        ],
        compiler_params=pltpu.CompilerParams(vmem_limit_bytes=36 * 1024 * 1024),
        cost_estimate=pl.CostEstimate(
            flops=flops,
            bytes_accessed=2 * (2 * rows.size + 2 * table.size + surface_rows.size),
            transcendentals=2 * columns * hidden,
        ),
        name="column_spectrum",
    )(
        quad_weight,
        rows,
        table,
        table_t,
        surface_rows,
        first,
        first_bias.reshape(1, hidden),
        mid,
        mid_bias.reshape(1, hidden),
        last,
    )


def exchange(chunks):
    return lax.all_to_all(chunks, "band", split_axis=0, concat_axis=0, tiled=True)


def fetch_kernel(ids_ref, held_ref, out_ref, wide, found):
    wide[...] = held_ref[...].astype(jnp.float32)
    count = ids_ref.shape[2]

    def one_peer(peer, carry):
        base = pl.multiple_of(peer * count, count)
        for i in range(count):
            found[pl.ds(base + i, 1), :] = wide[pl.ds(ids_ref[peer, 0, i], 1), :]
        return carry

    lax.fori_loop(0, ids_ref.shape[0], one_peer, 0)
    out_ref[...] = found[...].astype(out_ref.dtype)


def fetch_rows(ids, held):
    rows = ids.shape[0] * ids.shape[2]
    features = held.shape[1]
    return pl.pallas_call(
        fetch_kernel,
        in_specs=[pl.BlockSpec(memory_space=pltpu.SMEM), pl.BlockSpec(memory_space=pltpu.VMEM)],
        out_specs=pl.BlockSpec(memory_space=pltpu.VMEM),
        out_shape=jax.ShapeDtypeStruct((rows, features), held.dtype),
        scratch_shapes=[
            pltpu.VMEM(held.shape, jnp.float32),
            pltpu.VMEM((rows, features), jnp.float32),
        ],
        compiler_params=pltpu.CompilerParams(vmem_limit_bytes=VMEM_BYTES),
        cost_estimate=pl.CostEstimate(
            flops=0, bytes_accessed=20 * 2 * (held.size + rows * features), transcendentals=0
        ),
        name="fetch_rows",
    )(ids, held)


def place_piece(places_ref, first, quota, padded, wide, full_ref):
    def one_owner(owner, carry):
        base = pl.multiple_of(owner * padded, padded)
        for i in range(quota):
            full_ref[pl.ds(places_ref[first + owner, i], 1), :] = wide[pl.ds(base + i, 1), :]
        return carry

    lax.fori_loop(0, wide.shape[0] // padded, one_owner, 0)


def near_kernel(padded, places_ref, own_ref, above_ref, below_ref, full_ref, wide):
    owners = wide.shape[0] // padded
    for away, piece in ((0, own_ref), (1, above_ref), (3, below_ref)):
        wide[...] = piece[...].astype(jnp.float32)
        place_piece(places_ref, away * owners, places_ref.shape[1], padded, wide, full_ref)


def place_near(places, own, above, below, total):
    padded = own.shape[0] // (places.shape[0] // 4)
    features = own.shape[1]
    return pl.pallas_call(
        functools.partial(near_kernel, padded),
        in_specs=[pl.BlockSpec(memory_space=pltpu.SMEM)]
        + [pl.BlockSpec(memory_space=pltpu.VMEM)] * 3,
        out_specs=pl.BlockSpec(memory_space=pltpu.VMEM),
        out_shape=jax.ShapeDtypeStruct((total + 8, features), jnp.float32),
        scratch_shapes=[pltpu.VMEM(own.shape, jnp.float32)],
        compiler_params=pltpu.CompilerParams(vmem_limit_bytes=VMEM_BYTES),
        cost_estimate=pl.CostEstimate(flops=0, bytes_accessed=30 * 2**20, transcendentals=0),
        name="place_near",
    )(places, own, above, below)


def far_kernel(padded, places_ref, near_ref, first_ref, second_ref, out_ref, full, wide, rounded, sems):
    pieces = sems.shape[0] - 1
    size = out_ref.shape[0] // pieces
    copy = pltpu.make_async_copy(near_ref, full, sems.at[pieces])
    copy.start()
    half = first_ref.shape[0]
    wide[:half, :] = first_ref[...].astype(jnp.float32)
    wide[half:, :] = second_ref[...].astype(jnp.float32)
    copy.wait()
    owners = wide.shape[0] // padded
    place_piece(places_ref, 2 * owners, places_ref.shape[1], padded, wide, full)
    copies = []
    for i in range(pieces):
        rows = slice(i * size, (i + 1) * size)
        rounded[rows, :] = full[rows, :].astype(rounded.dtype)
        copies.append(
            pltpu.make_async_copy(
                rounded.at[pl.ds(i * size, size)], out_ref.at[pl.ds(i * size, size)], sems.at[i]
            )
        )
        copies[-1].start()
    for copy in copies:
        copy.wait()


def place_far(places, near, first, second, total):
    rows = first.shape[0] + second.shape[0]
    padded = rows // (places.shape[0] // 4)
    features = near.shape[1]
    return pl.pallas_call(
        functools.partial(far_kernel, padded),
        in_specs=[
            pl.BlockSpec(memory_space=pltpu.SMEM),
            pl.BlockSpec(memory_space=pl.ANY),
            pl.BlockSpec(memory_space=pltpu.VMEM),
            pl.BlockSpec(memory_space=pltpu.VMEM),
        ],
        out_specs=pl.BlockSpec(memory_space=pl.ANY),
        out_shape=jax.ShapeDtypeStruct((total, features), jnp.bfloat16),
        scratch_shapes=[
            pltpu.VMEM(near.shape, jnp.float32),
            pltpu.VMEM((rows, features), jnp.float32),
            pltpu.VMEM((total, features), jnp.bfloat16),
            pltpu.SemaphoreType.DMA((6,)),
        ],
        compiler_params=pltpu.CompilerParams(vmem_limit_bytes=VMEM_BYTES),
        cost_estimate=pl.CostEstimate(flops=0, bytes_accessed=20 * 2**20, transcendentals=0),
        name="place_far",
    )(places, near, first, second)


def gathered_over_members(places, piece, total, tables):
    members = lax.axis_size("ens")
    up = [(i, (i + 1) % members) for i in range(members)]
    down = [(i, (i - 1) % members) for i in range(members)]
    half = piece.shape[0] // 2
    below = lax.ppermute(piece, "ens", up)
    above = lax.ppermute(piece, "ens", down)
    below, above, tables = lax.optimization_barrier((below, above, tables))
    far_first = lax.ppermute(below[:half], "ens", up)
    far_second = lax.ppermute(above[half:], "ens", down)
    near = place_near(places, piece, above, below, total)
    return place_far(places, near, far_first, far_second, total), tables


def requests(dest_owner, dest_slot, held):
    owners = lax.axis_size("band")
    members = lax.axis_size("ens")
    total = dest_owner.size
    per_owner = total // owners
    quota = -(-per_owner // members)
    padded = -(-quota // 16) * 16
    columns = jnp.arange(total, dtype=jnp.int32)
    keys = (dest_owner * held + dest_slot).reshape(-1)
    keys, order = lax.sort((keys, columns), num_keys=1)
    slots = keys.reshape(owners, per_owner) - jnp.arange(owners, dtype=jnp.int32)[:, None] * held
    slots = jnp.pad(slots, ((0, 0), (0, quota * members - per_owner)))
    mine = lax.dynamic_slice_in_dim(slots, lax.axis_index("ens") * quota, quota, axis=1)
    mine = jnp.pad(mine, ((0, 0), (0, padded - quota)))
    return mine.reshape(owners, 1, padded), order


def places_of_rows(order, quota, longitudes):
    owners = lax.axis_size("band")
    members = lax.axis_size("ens")
    total = order.shape[0]
    per_owner = total // owners
    across = order % longitudes
    folded = jnp.where(across <= longitudes // 2, across, longitudes * 3 // 2 - across)
    order = order - across + folded
    places = jnp.pad(
        order.reshape(owners, per_owner),
        ((0, 0), (0, quota * members - per_owner)),
        constant_values=total,
    )
    places = places.reshape(owners, members, quota).transpose(1, 0, 2)
    places = jnp.concatenate([places, places], axis=0)
    places = lax.dynamic_slice_in_dim(places, lax.axis_index("ens"), members, axis=0)
    return places.reshape(members * owners, quota)


def local(
    spectral_state,
    lat_basis,
    quad_weight,
    wave_of_slot,
    dest_owner,
    dest_slot,
    surface,
    in_weight,
    surface_weight,
    in_bias,
    mid_weight,
    mid_bias,
    out_weight,
):
    bands = lax.axis_size("band")
    longitudes = dest_owner.shape[1]
    ids, order = requests(dest_owner, dest_slot, surface.shape[0])
    padded = ids.shape[2]
    quota = -(-(order.shape[0] // bands) // lax.axis_size("ens"))
    fourier = to_latitudes(lat_basis, spectral_state)
    replies = fetch_rows(exchange(ids), surface)
    replies, fourier = lax.optimization_barrier((replies, fourier))
    features = fourier.shape[1]
    fetched = exchange(replies.reshape(bands, padded, -1)).reshape(-1, surface.shape[1])
    places = places_of_rows(order, quota, longitudes)
    tables = fourier_tables(wave_of_slot, bands, longitudes)
    surface_rows, tables = gathered_over_members(places, fetched, order.shape[0], tables)
    banded = exchange(fourier.reshape(bands, -1, features)).reshape(-1, features)
    weight = quad_weight * math.sqrt(2.0 / longitudes)
    first = jnp.concatenate([in_weight, surface_weight], axis=0)
    network = (first, in_bias, mid_weight, mid_bias, out_weight)
    spectrum = column_spectrum(banded, tables, surface_rows, weight, bands, *network)
    owned = exchange(spectrum.reshape(bands, -1, features)).reshape(-1, features)
    return to_degrees(lat_basis, owned)


def solution(mesh):
    return jax.shard_map(
        local,
        mesh=mesh,
        in_specs=(
            P(("ens", "band"), None, None),
            P("band", None, None),
            P("band"),
            P(),
            P("band", None),
            P("band", None),
            P("band", None),
            P(),
            P(),
            P(),
            P(),
            P(),
            P(),
        ),
        out_specs=P(("ens", "band"), None, None),
        check_vma=False,
    )
```

```python
import functools
import math

import jax
import jax.numpy as jnp
from jax import lax
from jax.experimental import pallas as pl
from jax.experimental.pallas import tpu as pltpu
from jax.sharding import PartitionSpec as P

VMEM_BYTES = 24 * 1024 * 1024


def whole(shape):
    zeros = (0,) * len(shape)
    return pl.BlockSpec(shape, lambda *_: zeros)


def fourier_kernel(basis_ref, state_ref, out_ref, wide):
    slots, lats, features = pl.num_programs(0), basis_ref.shape[1], out_ref.shape[1]
    slot = pl.program_id(0)
    per_lat = out_ref.shape[0] // lats
    found = jnp.dot(basis_ref[0], state_ref[0], preferred_element_type=jnp.float32)
    for k in range(2):
        wide[pl.ds(2 * slot + k, lats, per_lat), :] = found[:, k * features : (k + 1) * features]

    @pl.when(slot == slots - 1)
    def _():
        out_ref[...] = wide[...].astype(out_ref.dtype)


def to_latitudes(lat_basis, spectral_state):
    slots, lats, degrees = lat_basis.shape
    features = spectral_state.shape[2] // 2
    rows = lats * slots * 2
    return pl.pallas_call(
        fourier_kernel,
        grid=(slots,),
        in_specs=[
            pl.BlockSpec((1, lats, degrees), lambda s: (s, 0, 0)),
            pl.BlockSpec((1, degrees, 2 * features), lambda s: (s, 0, 0)),
        ],
        out_specs=whole((rows, features)),
        out_shape=jax.ShapeDtypeStruct((rows, features), jnp.bfloat16),
        scratch_shapes=[pltpu.VMEM((rows, features), jnp.float32)],
        compiler_params=pltpu.CompilerParams(vmem_limit_bytes=VMEM_BYTES),
        cost_estimate=pl.CostEstimate(
            flops=2 * slots * lats * degrees * 2 * features,
            bytes_accessed=2 * (lat_basis.size + spectral_state.size + rows * features),
            transcendentals=0,
        ),
        name="to_latitudes",
    )(lat_basis, spectral_state)


def degrees_kernel(basis_ref, rows_ref, out_ref, wide):
    lats = basis_ref.shape[1]
    slot = pl.program_id(0)
    per_lat = rows_ref.shape[0] // lats

    @pl.when(slot == 0)
    def _():
        wide[...] = rows_ref[...].astype(jnp.float32)

    spectrum = jnp.concatenate(
        [wide[pl.ds(2 * slot + k, lats, per_lat), :].astype(jnp.bfloat16) for k in range(2)],
        axis=1,
    )
    out_ref[0] = lax.dot_general(
        basis_ref[0], spectrum, (((0,), (0,)), ((), ())), preferred_element_type=jnp.float32
    )


def to_degrees(lat_basis, rows):
    slots, lats, degrees = lat_basis.shape
    features = rows.shape[1]
    return pl.pallas_call(
        degrees_kernel,
        grid=(slots,),
        in_specs=[
            pl.BlockSpec((1, lats, degrees), lambda s: (s, 0, 0)),
            whole(rows.shape),
        ],
        out_specs=pl.BlockSpec((1, degrees, 2 * features), lambda s: (s, 0, 0)),
        out_shape=jax.ShapeDtypeStruct((slots, degrees, 2 * features), jnp.float32),
        scratch_shapes=[pltpu.VMEM(rows.shape, jnp.float32)],
        compiler_params=pltpu.CompilerParams(vmem_limit_bytes=VMEM_BYTES),
        cost_estimate=pl.CostEstimate(
            flops=2 * slots * lats * degrees * 2 * features,
            bytes_accessed=2 * (lat_basis.size + rows.size) + 8 * slots * degrees * features,
            transcendentals=0,
        ),
        name="to_degrees",
    )(lat_basis, rows)


def angle_parts(waves, step, count, quarter, longitudes, axis):
    positions = jnp.arange(count, dtype=jnp.int32) * step
    shape = (-1, 1) if axis == 1 else (1, -1)
    phases = waves.reshape(shape) * positions.reshape(shape[::-1])
    phases = (phases + quarter.reshape(shape)) % longitudes
    angles = phases.astype(jnp.float32) * (2.0 * math.pi / longitudes)
    return jnp.cos(angles), jnp.sin(angles)


def table_kernel(hi_cos, hi_sin, lo_cos, lo_sin, hi_cos_t, hi_sin_t, lo_cos_t, lo_sin_t, out, out_t):
    longitudes = out.shape[1]
    width = lo_cos.shape[1]
    for a in range(hi_cos.shape[1]):
        size = min(width, longitudes - a * width)
        block = hi_cos[:, a : a + 1] * lo_cos[...] - hi_sin[:, a : a + 1] * lo_sin[...]
        out[:, a * width : a * width + size] = block[:, :size].astype(out.dtype)
    height = lo_cos_t.shape[0]
    for a in range(hi_cos_t.shape[0]):
        block = hi_cos_t[a : a + 1, :] * lo_cos_t[...] - hi_sin_t[a : a + 1, :] * lo_sin_t[...]
        out_t[a * height : (a + 1) * height, :] = block.astype(out_t.dtype)


def fourier_tables(wave_of_slot, sources, longitudes):
    per_source = wave_of_slot.shape[0] // sources
    waves = (wave_of_slot + 1).reshape(sources, per_source).T.reshape(-1)
    waves = jnp.concatenate([waves, waves])
    terms = waves.shape[0]
    quarter = jnp.arange(terms, dtype=jnp.int32) // (terms // 2) * (longitudes // 4)
    none = jnp.zeros_like(quarter)
    width, height = 128, 32
    kept = -(-(longitudes // 2 + 1) // height) * height
    wide = angle_parts(waves, width, -(-kept // width), quarter, longitudes, 1)
    wide += angle_parts(waves, 1, width, none, longitudes, 1)
    tall = angle_parts(waves, height, kept // height, quarter, longitudes, 0)
    tall += angle_parts(waves, 1, height, none, longitudes, 0)
    return pl.pallas_call(
        table_kernel,
        out_shape=(
            jax.ShapeDtypeStruct((terms, kept), jnp.bfloat16),
            jax.ShapeDtypeStruct((kept, terms), jnp.bfloat16),
        ),
        compiler_params=pltpu.CompilerParams(vmem_limit_bytes=VMEM_BYTES),
        cost_estimate=pl.CostEstimate(
            flops=6 * terms * kept, bytes_accessed=4 * terms * kept, transcendentals=0
        ),
        name="fourier_tables",
    )(*wide, *tall)


def silu(v):
    half = 0.5 * v
    return half + half * jnp.tanh(half)


def columns_kernel(
    sources,
    weight_ref,
    places_ref,
    far_first_ref,
    far_second_ref,
    rows_ref,
    table_ref,
    table_t_ref,
    near_ref,
    first_ref,
    first_bias_ref,
    mid_ref,
    mid_bias_ref,
    last_ref,
    out_ref,
    wide_in,
    wide_out,
    coefficients,
    evens,
    odds,
    far_full,
):
    step = pl.program_id(0)
    features = rows_ref.shape[1]
    terms = table_ref.shape[0] // sources
    kept = table_ref.shape[1]
    stride = rows_ref.shape[0] // sources
    lanes = coefficients.shape[1]
    group = lanes // features
    half = near_ref.shape[0] // group // 2
    split = table_ref.shape[0] // 2

    @pl.when(step == 0)
    def _():
        wide_in[...] = rows_ref[...].astype(jnp.float32)
        far_full[...] = jnp.zeros_like(far_full)
        far_half = far_first_ref.shape[0]
        far = wide_out.at[pl.ds(0, 2 * far_half)]
        far[:far_half, :] = far_first_ref[...].astype(jnp.float32)
        far[far_half:, :] = far_second_ref[...].astype(jnp.float32)
        owners = places_ref.shape[0] // 4
        padded = 2 * far_half // owners
        place_piece(places_ref, 2 * owners, places_ref.shape[1], padded, far, far_full)

    def place_of(q):
        return (q % 2) * split + q // 2 * sources

    for j in range(group):
        lat = step * group + j
        for q in range(terms):
            at = place_of(q)
            coefficients[at : at + sources, j * features : (j + 1) * features] = wide_in[
                pl.ds(terms * lat + q, sources, stride), :
            ].astype(jnp.bfloat16)

    def network(state, start):
        def surface_at(j):
            here = 2 * half * j + start
            at = pl.multiple_of(step * group * 2 * half + here, 16)
            near = near_ref[here : here + half, :].astype(jnp.float32)
            return (near + far_full[pl.ds(at, half), :]).astype(jnp.bfloat16)

        joined = jnp.concatenate(
            [
                jnp.concatenate(
                    [
                        state[:, j * features : (j + 1) * features].astype(jnp.bfloat16),
                        surface_at(j),
                    ],
                    axis=1,
                )
                for j in range(group)
            ],
            axis=0,
        )
        first = jnp.dot(joined, first_ref[...], preferred_element_type=jnp.float32)
        first = silu(first + first_bias_ref[...]).astype(jnp.bfloat16)
        second = jnp.dot(first, mid_ref[...], preferred_element_type=jnp.float32)
        second = silu(second + mid_bias_ref[...]).astype(jnp.bfloat16)
        third = jnp.dot(second, last_ref[...], preferred_element_type=jnp.float32)
        return jnp.concatenate([third[j * half : (j + 1) * half, :] for j in range(group)], axis=1)

    even = jnp.dot(
        table_t_ref[:, :split], coefficients[:split, :], preferred_element_type=jnp.float32
    )
    odd = jnp.dot(
        table_t_ref[:half, split:], coefficients[split:, :], preferred_element_type=jnp.float32
    )
    lone, even = even[half : half + 1, :], even[:half, :]
    top = lax.broadcasted_iota(jnp.int32, (half, lanes), 0) == 0
    east = network(even + odd, 0)
    west = network(jnp.where(top, lone, even - odd), half)
    evens[:half, :] = jnp.where(top, east, east + west).astype(jnp.bfloat16)
    evens[half:, :] = jnp.where(top[: kept - half, :], west[: kept - half, :], 0.0).astype(
        jnp.bfloat16
    )
    odds[:half, :] = (east - west).astype(jnp.bfloat16)
    odds[half:, :] = jnp.zeros((kept - half, lanes), jnp.bfloat16)

    for k, halves in enumerate((evens, odds)):
        spectrum = jnp.dot(
            table_ref[k * split : (k + 1) * split, :],
            halves[...],
            preferred_element_type=jnp.float32,
        )
        for j in range(group):
            lat = step * group + j
            scaled = spectrum[:, j * features : (j + 1) * features] * weight_ref[lat]
            for q in range(k, terms, 2):
                at = q // 2 * sources
                wide_out[pl.ds(terms * lat + q, sources, stride), :] = scaled[at : at + sources, :]

    @pl.when(step == pl.num_programs(0) - 1)
    def _():
        out_ref[...] = wide_out[...].astype(out_ref.dtype)


def column_spectrum(
    rows, tables, surface_rows, quad_weight, sources, first, first_bias, mid, mid_bias, last
):
    table, table_t = tables
    terms, kept = table.shape
    places, near, far_first, far_second = surface_rows
    longitudes = near.shape[0] // quad_weight.shape[0]
    features = rows.shape[1]
    lats = quad_weight.shape[0]
    group = 2 if lats % 2 == 0 else 1
    hidden = first.shape[1]
    columns = lats * longitudes
    flops = 2 * columns * (terms * features + 2 * features * hidden)
    flops += 2 * columns * (hidden * hidden + hidden * features)
    return pl.pallas_call(
        functools.partial(columns_kernel, sources),
        grid=(lats // group,),
        in_specs=[
            pl.BlockSpec(memory_space=pltpu.SMEM),
            pl.BlockSpec(memory_space=pltpu.SMEM),
            whole(far_first.shape),
            whole(far_second.shape),
            whole(rows.shape),
            whole(table.shape),
            whole(table_t.shape),
            pl.BlockSpec((group * longitudes, near.shape[1]), lambda i: (i, 0)),
            whole(first.shape),
            whole((1, hidden)),
            whole(mid.shape),
            whole((1, hidden)),
            whole(last.shape),
        ],
        out_specs=whole(rows.shape),
        out_shape=jax.ShapeDtypeStruct(rows.shape, jnp.bfloat16),
        scratch_shapes=[
            pltpu.VMEM(rows.shape, jnp.float32),
            pltpu.VMEM(rows.shape, jnp.float32),
            pltpu.VMEM((terms, group * features), jnp.bfloat16),
            pltpu.VMEM((kept, group * features), jnp.bfloat16),
            pltpu.VMEM((kept, group * features), jnp.bfloat16),
            pltpu.VMEM((near.shape[0] + 8, near.shape[1]), jnp.float32),
        ],
        compiler_params=pltpu.CompilerParams(vmem_limit_bytes=60 * 1024 * 1024),
        cost_estimate=pl.CostEstimate(
            flops=flops,
            bytes_accessed=2 * (2 * rows.size + 2 * table.size + near.size),
            transcendentals=2 * columns * hidden,
        ),
        name="column_spectrum",
    )(
        quad_weight,
        places,
        far_first,
        far_second,
        rows,
        table,
        table_t,
        near,
        first,
        first_bias.reshape(1, hidden),
        mid,
        mid_bias.reshape(1, hidden),
        last,
    )


def exchange(chunks):
    return lax.all_to_all(chunks, "band", split_axis=0, concat_axis=0, tiled=True)


def fetch_kernel(ids_ref, held_ref, out_ref, wide, found):
    wide[...] = held_ref[...].astype(jnp.float32)
    count = ids_ref.shape[2]

    def one_peer(peer, carry):
        base = pl.multiple_of(peer * count, count)
        for i in range(count):
            found[pl.ds(base + i, 1), :] = wide[pl.ds(ids_ref[peer, 0, i], 1), :]
        return carry

    lax.fori_loop(0, ids_ref.shape[0], one_peer, 0)
    out_ref[...] = found[...].astype(out_ref.dtype)


def fetch_rows(ids, held):
    rows = ids.shape[0] * ids.shape[2]
    features = held.shape[1]
    return pl.pallas_call(
        fetch_kernel,
        in_specs=[pl.BlockSpec(memory_space=pltpu.SMEM), pl.BlockSpec(memory_space=pltpu.VMEM)],
        out_specs=pl.BlockSpec(memory_space=pltpu.VMEM),
        out_shape=jax.ShapeDtypeStruct((rows, features), held.dtype),
        scratch_shapes=[
            pltpu.VMEM(held.shape, jnp.float32),
            pltpu.VMEM((rows, features), jnp.float32),
        ],
        compiler_params=pltpu.CompilerParams(vmem_limit_bytes=VMEM_BYTES),
        cost_estimate=pl.CostEstimate(
            flops=0, bytes_accessed=20 * 2 * (held.size + rows * features), transcendentals=0
        ),
        name="fetch_rows",
    )(ids, held)


def place_piece(places_ref, first, quota, padded, wide, full_ref):
    def one_owner(owner, carry):
        base = pl.multiple_of(owner * padded, padded)
        for i in range(quota):
            full_ref[pl.ds(places_ref[first + owner, i], 1), :] = wide[pl.ds(base + i, 1), :]
        return carry

    lax.fori_loop(0, wide.shape[0] // padded, one_owner, 0)


def near_kernel(padded, places_ref, own_ref, above_ref, below_ref, out_ref, full, wide):
    owners = wide.shape[0] // padded
    full[...] = jnp.zeros_like(full)
    for away, piece in ((0, own_ref), (1, above_ref), (3, below_ref)):
        wide[...] = piece[...].astype(jnp.float32)
        place_piece(places_ref, away * owners, places_ref.shape[1], padded, wide, full)
    out_ref[...] = full[: out_ref.shape[0], :].astype(out_ref.dtype)


def place_near(places, own, above, below, total):
    padded = own.shape[0] // (places.shape[0] // 4)
    features = own.shape[1]
    return pl.pallas_call(
        functools.partial(near_kernel, padded),
        in_specs=[pl.BlockSpec(memory_space=pltpu.SMEM)]
        + [pl.BlockSpec(memory_space=pltpu.VMEM)] * 3,
        out_specs=pl.BlockSpec(memory_space=pltpu.VMEM),
        out_shape=jax.ShapeDtypeStruct((total, features), own.dtype),
        scratch_shapes=[
            pltpu.VMEM((total + 8, features), jnp.float32),
            pltpu.VMEM(own.shape, jnp.float32),
        ],
        compiler_params=pltpu.CompilerParams(vmem_limit_bytes=VMEM_BYTES),
        cost_estimate=pl.CostEstimate(flops=0, bytes_accessed=30 * 2**20, transcendentals=0),
        name="place_near",
    )(places, own, above, below)


def gathered_over_members(places, piece, total, tables):
    members = lax.axis_size("ens")
    up = [(i, (i + 1) % members) for i in range(members)]
    down = [(i, (i - 1) % members) for i in range(members)]
    half = piece.shape[0] // 2
    below = lax.ppermute(piece, "ens", up)
    above = lax.ppermute(piece, "ens", down)
    below, above, tables = lax.optimization_barrier((below, above, tables))
    far_first = lax.ppermute(below[:half], "ens", up)
    far_second = lax.ppermute(above[half:], "ens", down)
    near = place_near(places, piece, above, below, total)
    return (places, near, far_first, far_second), tables


def requests(dest_owner, dest_slot, held):
    owners = lax.axis_size("band")
    members = lax.axis_size("ens")
    total = dest_owner.size
    per_owner = total // owners
    quota = -(-per_owner // members)
    padded = -(-quota // 16) * 16
    columns = jnp.arange(total, dtype=jnp.int32)
    keys = (dest_owner * held + dest_slot).reshape(-1)
    keys, order = lax.sort((keys, columns), num_keys=1)
    slots = keys.reshape(owners, per_owner) - jnp.arange(owners, dtype=jnp.int32)[:, None] * held
    slots = jnp.pad(slots, ((0, 0), (0, quota * members - per_owner)))
    mine = lax.dynamic_slice_in_dim(slots, lax.axis_index("ens") * quota, quota, axis=1)
    mine = jnp.pad(mine, ((0, 0), (0, padded - quota)))
    return mine.reshape(owners, 1, padded), order


def places_of_rows(order, quota, longitudes):
    owners = lax.axis_size("band")
    members = lax.axis_size("ens")
    total = order.shape[0]
    per_owner = total // owners
    across = order % longitudes
    folded = jnp.where(across <= longitudes // 2, across, longitudes * 3 // 2 - across)
    order = order - across + folded
    places = jnp.pad(
        order.reshape(owners, per_owner),
        ((0, 0), (0, quota * members - per_owner)),
        constant_values=total,
    )
    places = places.reshape(owners, members, quota).transpose(1, 0, 2)
    places = jnp.concatenate([places, places], axis=0)
    places = lax.dynamic_slice_in_dim(places, lax.axis_index("ens"), members, axis=0)
    return places.reshape(members * owners, quota)


def local(
    spectral_state,
    lat_basis,
    quad_weight,
    wave_of_slot,
    dest_owner,
    dest_slot,
    surface,
    in_weight,
    surface_weight,
    in_bias,
    mid_weight,
    mid_bias,
    out_weight,
):
    bands = lax.axis_size("band")
    longitudes = dest_owner.shape[1]
    ids, order = requests(dest_owner, dest_slot, surface.shape[0])
    padded = ids.shape[2]
    quota = -(-(order.shape[0] // bands) // lax.axis_size("ens"))
    fourier = to_latitudes(lat_basis, spectral_state)
    replies = fetch_rows(exchange(ids), surface)
    replies, fourier = lax.optimization_barrier((replies, fourier))
    features = fourier.shape[1]
    fetched = exchange(replies.reshape(bands, padded, -1)).reshape(-1, surface.shape[1])
    places = places_of_rows(order, quota, longitudes)
    tables = fourier_tables(wave_of_slot, bands, longitudes)
    surface_rows, tables = gathered_over_members(places, fetched, order.shape[0], tables)
    banded = exchange(fourier.reshape(bands, -1, features)).reshape(-1, features)
    weight = quad_weight * math.sqrt(2.0 / longitudes)
    first = jnp.concatenate([in_weight, surface_weight], axis=0)
    network = (first, in_bias, mid_weight, mid_bias, out_weight)
    spectrum = column_spectrum(banded, tables, surface_rows, weight, bands, *network)
    owned = exchange(spectrum.reshape(bands, -1, features)).reshape(-1, features)
    return to_degrees(lat_basis, owned)


def solution(mesh):
    return jax.shard_map(
        local,
        mesh=mesh,
        in_specs=(
            P(("ens", "band"), None, None),
            P("band", None, None),
            P("band"),
            P(),
            P("band", None),
            P("band", None),
            P("band", None),
            P(),
            P(),
            P(),
            P(),
            P(),
            P(),
        ),
        out_specs=P(("ens", "band"), None, None),
        check_vma=False,
    )
```

```python
import functools
import math

import jax
import jax.numpy as jnp
from jax import lax
from jax.experimental import pallas as pl
from jax.experimental.pallas import tpu as pltpu
from jax.sharding import PartitionSpec as P

VMEM_BYTES = 24 * 1024 * 1024


def whole(shape):
    zeros = (0,) * len(shape)
    return pl.BlockSpec(shape, lambda *_: zeros)


def fourier_kernel(basis_ref, state_ref, out_ref, wide):
    slots, lats, features = pl.num_programs(0), basis_ref.shape[1], out_ref.shape[1]
    slot = pl.program_id(0)
    per_lat = out_ref.shape[0] // lats
    found = jnp.dot(basis_ref[0], state_ref[0], preferred_element_type=jnp.float32)
    for k in range(2):
        wide[pl.ds(2 * slot + k, lats, per_lat), :] = found[:, k * features : (k + 1) * features]

    @pl.when(slot == slots - 1)
    def _():
        out_ref[...] = wide[...].astype(out_ref.dtype)


def to_latitudes(lat_basis, spectral_state):
    slots, lats, degrees = lat_basis.shape
    features = spectral_state.shape[2] // 2
    rows = lats * slots * 2
    return pl.pallas_call(
        fourier_kernel,
        grid=(slots,),
        in_specs=[
            pl.BlockSpec((1, lats, degrees), lambda s: (s, 0, 0)),
            pl.BlockSpec((1, degrees, 2 * features), lambda s: (s, 0, 0)),
        ],
        out_specs=whole((rows, features)),
        out_shape=jax.ShapeDtypeStruct((rows, features), jnp.bfloat16),
        scratch_shapes=[pltpu.VMEM((rows, features), jnp.float32)],
        compiler_params=pltpu.CompilerParams(vmem_limit_bytes=VMEM_BYTES),
        cost_estimate=pl.CostEstimate(
            flops=2 * slots * lats * degrees * 2 * features,
            bytes_accessed=2 * (lat_basis.size + spectral_state.size + rows * features),
            transcendentals=0,
        ),
        name="to_latitudes",
    )(lat_basis, spectral_state)


def degrees_kernel(basis_ref, rows_ref, out_ref, wide):
    lats = basis_ref.shape[1]
    slot = pl.program_id(0)
    per_lat = rows_ref.shape[0] // lats

    @pl.when(slot == 0)
    def _():
        wide[...] = rows_ref[...].astype(jnp.float32)

    spectrum = jnp.concatenate(
        [wide[pl.ds(2 * slot + k, lats, per_lat), :].astype(jnp.bfloat16) for k in range(2)],
        axis=1,
    )
    out_ref[0] = lax.dot_general(
        basis_ref[0], spectrum, (((0,), (0,)), ((), ())), preferred_element_type=jnp.float32
    )


def to_degrees(lat_basis, rows):
    slots, lats, degrees = lat_basis.shape
    features = rows.shape[1]
    return pl.pallas_call(
        degrees_kernel,
        grid=(slots,),
        in_specs=[
            pl.BlockSpec((1, lats, degrees), lambda s: (s, 0, 0)),
            pl.BlockSpec(memory_space=pltpu.VMEM),
        ],
        out_specs=pl.BlockSpec((1, degrees, 2 * features), lambda s: (s, 0, 0)),
        out_shape=jax.ShapeDtypeStruct((slots, degrees, 2 * features), jnp.float32),
        scratch_shapes=[pltpu.VMEM(rows.shape, jnp.float32)],
        compiler_params=pltpu.CompilerParams(vmem_limit_bytes=VMEM_BYTES),
        cost_estimate=pl.CostEstimate(
            flops=2 * slots * lats * degrees * 2 * features,
            bytes_accessed=2 * (lat_basis.size + rows.size) + 8 * slots * degrees * features,
            transcendentals=0,
        ),
        name="to_degrees",
    )(lat_basis, rows)


def angle_parts(waves, step, count, quarter, longitudes, axis):
    positions = jnp.arange(count, dtype=jnp.int32) * step
    shape = (-1, 1) if axis == 1 else (1, -1)
    phases = waves.reshape(shape) * positions.reshape(shape[::-1])
    phases = (phases + quarter.reshape(shape)) % longitudes
    angles = phases.astype(jnp.float32) * (2.0 * math.pi / longitudes)
    return jnp.cos(angles), jnp.sin(angles)


def table_kernel(hi_cos, hi_sin, lo_cos, lo_sin, hi_cos_t, hi_sin_t, lo_cos_t, lo_sin_t, out, out_t):
    longitudes = out.shape[1]
    width = lo_cos.shape[1]
    for a in range(hi_cos.shape[1]):
        size = min(width, longitudes - a * width)
        block = hi_cos[:, a : a + 1] * lo_cos[...] - hi_sin[:, a : a + 1] * lo_sin[...]
        out[:, a * width : a * width + size] = block[:, :size].astype(out.dtype)
    height = lo_cos_t.shape[0]
    for a in range(hi_cos_t.shape[0]):
        block = hi_cos_t[a : a + 1, :] * lo_cos_t[...] - hi_sin_t[a : a + 1, :] * lo_sin_t[...]
        out_t[a * height : (a + 1) * height, :] = block.astype(out_t.dtype)


def fourier_tables(wave_of_slot, sources, longitudes):
    per_source = wave_of_slot.shape[0] // sources
    waves = (wave_of_slot + 1).reshape(sources, per_source).T.reshape(-1)
    waves = jnp.concatenate([waves, waves])
    terms = waves.shape[0]
    quarter = jnp.arange(terms, dtype=jnp.int32) // (terms // 2) * (longitudes // 4)
    none = jnp.zeros_like(quarter)
    width, height = 128, 32
    kept = -(-(longitudes // 2 + 1) // height) * height
    wide = angle_parts(waves, width, -(-kept // width), quarter, longitudes, 1)
    wide += angle_parts(waves, 1, width, none, longitudes, 1)
    tall = angle_parts(waves, height, kept // height, quarter, longitudes, 0)
    tall += angle_parts(waves, 1, height, none, longitudes, 0)
    return pl.pallas_call(
        table_kernel,
        out_shape=(
            jax.ShapeDtypeStruct((terms, kept), jnp.bfloat16),
            jax.ShapeDtypeStruct((kept, terms), jnp.bfloat16),
        ),
        compiler_params=pltpu.CompilerParams(vmem_limit_bytes=VMEM_BYTES),
        cost_estimate=pl.CostEstimate(
            flops=6 * terms * kept, bytes_accessed=4 * terms * kept, transcendentals=0
        ),
        name="fourier_tables",
    )(*wide, *tall)


def silu(v):
    half = 0.5 * v
    return half + half * jnp.tanh(half)


def columns_kernel(
    sources,
    weight_ref,
    places_ref,
    far_first_ref,
    far_second_ref,
    rows_ref,
    table_ref,
    table_t_ref,
    near_ref,
    first_ref,
    first_bias_ref,
    mid_ref,
    mid_bias_ref,
    last_ref,
    out_ref,
    wide_in,
    wide_out,
    coefficients,
    evens,
    odds,
    far_full,
):
    step = pl.program_id(0)
    features = rows_ref.shape[1]
    terms = table_ref.shape[0] // sources
    kept = table_ref.shape[1]
    stride = rows_ref.shape[0] // sources
    lanes = coefficients.shape[1]
    group = lanes // features
    half = near_ref.shape[0] // group // 2
    split = table_ref.shape[0] // 2

    @pl.when(step == 0)
    def _():
        wide_in[...] = rows_ref[...].astype(jnp.float32)
        far_full[...] = jnp.zeros_like(far_full)
        far_half = far_first_ref.shape[0]
        far = wide_out.at[pl.ds(0, 2 * far_half)]
        far[:far_half, :] = far_first_ref[...].astype(jnp.float32)
        far[far_half:, :] = far_second_ref[...].astype(jnp.float32)
        owners = places_ref.shape[0] // 4
        padded = 2 * far_half // owners
        place_piece(places_ref, 2 * owners, places_ref.shape[1], padded, far, far_full)

    def place_of(q):
        return (q % 2) * split + q // 2 * sources

    for j in range(group):
        lat = step * group + j
        for q in range(terms):
            at = place_of(q)
            coefficients[at : at + sources, j * features : (j + 1) * features] = wide_in[
                pl.ds(terms * lat + q, sources, stride), :
            ].astype(jnp.bfloat16)

    def network(state, start):
        def surface_at(j):
            here = 2 * half * j + start
            at = pl.multiple_of(step * group * 2 * half + here, 16)
            near = near_ref[here : here + half, :].astype(jnp.float32)
            return (near + far_full[pl.ds(at, half), :]).astype(jnp.bfloat16)

        joined = jnp.concatenate(
            [
                jnp.concatenate(
                    [
                        state[:, j * features : (j + 1) * features].astype(jnp.bfloat16),
                        surface_at(j),
                    ],
                    axis=1,
                )
                for j in range(group)
            ],
            axis=0,
        )
        first = jnp.dot(joined, first_ref[...], preferred_element_type=jnp.float32)
        first = silu(first + first_bias_ref[...]).astype(jnp.bfloat16)
        second = jnp.dot(first, mid_ref[...], preferred_element_type=jnp.float32)
        second = silu(second + mid_bias_ref[...]).astype(jnp.bfloat16)
        third = jnp.dot(second, last_ref[...], preferred_element_type=jnp.float32)
        return jnp.concatenate([third[j * half : (j + 1) * half, :] for j in range(group)], axis=1)

    even = jnp.dot(
        table_t_ref[:, :split], coefficients[:split, :], preferred_element_type=jnp.float32
    )
    odd = jnp.dot(
        table_t_ref[:half, split:], coefficients[split:, :], preferred_element_type=jnp.float32
    )
    lone, even = even[half : half + 1, :], even[:half, :]
    top = lax.broadcasted_iota(jnp.int32, (half, lanes), 0) == 0
    east = network(even + odd, 0)
    west = network(jnp.where(top, lone, even - odd), half)
    evens[:half, :] = jnp.where(top, east, east + west).astype(jnp.bfloat16)
    evens[half:, :] = jnp.where(top[: kept - half, :], west[: kept - half, :], 0.0).astype(
        jnp.bfloat16
    )
    odds[:half, :] = (east - west).astype(jnp.bfloat16)
    odds[half:, :] = jnp.zeros((kept - half, lanes), jnp.bfloat16)

    for k, halves in enumerate((evens, odds)):
        spectrum = jnp.dot(
            table_ref[k * split : (k + 1) * split, :],
            halves[...],
            preferred_element_type=jnp.float32,
        )
        for j in range(group):
            lat = step * group + j
            scaled = spectrum[:, j * features : (j + 1) * features] * weight_ref[lat]
            for q in range(k, terms, 2):
                at = q // 2 * sources
                wide_out[pl.ds(terms * lat + q, sources, stride), :] = scaled[at : at + sources, :]

    @pl.when(step == pl.num_programs(0) - 1)
    def _():
        out_ref[...] = wide_out[...].astype(out_ref.dtype)


def column_spectrum(
    rows, tables, surface_rows, quad_weight, sources, first, first_bias, mid, mid_bias, last
):
    table, table_t = tables
    terms, kept = table.shape
    places, near, far_first, far_second = surface_rows
    longitudes = near.shape[0] // quad_weight.shape[0]
    features = rows.shape[1]
    lats = quad_weight.shape[0]
    group = 2 if lats % 2 == 0 else 1
    hidden = first.shape[1]
    columns = lats * longitudes
    flops = 2 * columns * (terms * features + 2 * features * hidden)
    flops += 2 * columns * (hidden * hidden + hidden * features)
    return pl.pallas_call(
        functools.partial(columns_kernel, sources),
        grid=(lats // group,),
        in_specs=[
            pl.BlockSpec(memory_space=pltpu.SMEM),
            pl.BlockSpec(memory_space=pltpu.SMEM),
            whole(far_first.shape),
            whole(far_second.shape),
            whole(rows.shape),
            whole(table.shape),
            whole(table_t.shape),
            pl.BlockSpec((group * longitudes, near.shape[1]), lambda i: (i, 0)),
            whole(first.shape),
            whole((1, hidden)),
            whole(mid.shape),
            whole((1, hidden)),
            whole(last.shape),
        ],
        out_specs=whole(rows.shape),
        out_shape=jax.ShapeDtypeStruct(rows.shape, jnp.bfloat16),
        scratch_shapes=[
            pltpu.VMEM(rows.shape, jnp.float32),
            pltpu.VMEM(rows.shape, jnp.float32),
            pltpu.VMEM((terms, group * features), jnp.bfloat16),
            pltpu.VMEM((kept, group * features), jnp.bfloat16),
            pltpu.VMEM((kept, group * features), jnp.bfloat16),
            pltpu.VMEM((near.shape[0] + 8, near.shape[1]), jnp.float32),
        ],
        compiler_params=pltpu.CompilerParams(vmem_limit_bytes=60 * 1024 * 1024),
        cost_estimate=pl.CostEstimate(
            flops=flops,
            bytes_accessed=2 * (2 * rows.size + 2 * table.size + near.size),
            transcendentals=2 * columns * hidden,
        ),
        name="column_spectrum",
    )(
        quad_weight,
        places,
        far_first,
        far_second,
        rows,
        table,
        table_t,
        near,
        first,
        first_bias.reshape(1, hidden),
        mid,
        mid_bias.reshape(1, hidden),
        last,
    )


def exchange(chunks):
    return lax.all_to_all(chunks, "band", split_axis=0, concat_axis=0, tiled=True)


def fetch_kernel(ids_ref, held_ref, out_ref, wide, found):
    wide[...] = held_ref[...].astype(jnp.float32)
    count = ids_ref.shape[2]

    def one_peer(peer, carry):
        base = pl.multiple_of(peer * count, count)
        for i in range(count):
            found[pl.ds(base + i, 1), :] = wide[pl.ds(ids_ref[peer, 0, i], 1), :]
        return carry

    lax.fori_loop(0, ids_ref.shape[0], one_peer, 0)
    out_ref[...] = found[...].astype(out_ref.dtype)


def fetch_rows(ids, held):
    rows = ids.shape[0] * ids.shape[2]
    features = held.shape[1]
    return pl.pallas_call(
        fetch_kernel,
        in_specs=[pl.BlockSpec(memory_space=pltpu.SMEM), pl.BlockSpec(memory_space=pltpu.VMEM)],
        out_specs=pl.BlockSpec(memory_space=pltpu.VMEM),
        out_shape=jax.ShapeDtypeStruct((rows, features), held.dtype),
        scratch_shapes=[
            pltpu.VMEM(held.shape, jnp.float32),
            pltpu.VMEM((rows, features), jnp.float32),
        ],
        compiler_params=pltpu.CompilerParams(vmem_limit_bytes=VMEM_BYTES),
        cost_estimate=pl.CostEstimate(
            flops=0, bytes_accessed=20 * 2 * (held.size + rows * features), transcendentals=0
        ),
        name="fetch_rows",
    )(ids, held)


def place_piece(places_ref, first, quota, padded, wide, full_ref):
    def one_owner(owner, carry):
        base = pl.multiple_of(owner * padded, padded)
        for i in range(quota):
            full_ref[pl.ds(places_ref[first + owner, i], 1), :] = wide[pl.ds(base + i, 1), :]
        return carry

    lax.fori_loop(0, wide.shape[0] // padded, one_owner, 0)


def near_kernel(padded, places_ref, own_ref, above_ref, below_ref, out_ref, full, wide):
    owners = wide.shape[0] // padded
    full[...] = jnp.zeros_like(full)
    for away, piece in ((0, own_ref), (1, above_ref), (3, below_ref)):
        wide[...] = piece[...].astype(jnp.float32)
        place_piece(places_ref, away * owners, places_ref.shape[1], padded, wide, full)
    out_ref[...] = full[: out_ref.shape[0], :].astype(out_ref.dtype)


def place_near(places, own, above, below, total):
    padded = own.shape[0] // (places.shape[0] // 4)
    features = own.shape[1]
    return pl.pallas_call(
        functools.partial(near_kernel, padded),
        in_specs=[pl.BlockSpec(memory_space=pltpu.SMEM)]
        + [pl.BlockSpec(memory_space=pltpu.VMEM)] * 3,
        out_specs=pl.BlockSpec(memory_space=pltpu.VMEM),
        out_shape=jax.ShapeDtypeStruct((total, features), own.dtype),
        scratch_shapes=[
            pltpu.VMEM((total + 8, features), jnp.float32),
            pltpu.VMEM(own.shape, jnp.float32),
        ],
        compiler_params=pltpu.CompilerParams(vmem_limit_bytes=VMEM_BYTES),
        cost_estimate=pl.CostEstimate(flops=0, bytes_accessed=30 * 2**20, transcendentals=0),
        name="place_near",
    )(places, own, above, below)


def gathered_over_members(places, piece, total, tables):
    members = lax.axis_size("ens")
    up = [(i, (i + 1) % members) for i in range(members)]
    down = [(i, (i - 1) % members) for i in range(members)]
    half = piece.shape[0] // 2
    below = lax.ppermute(piece, "ens", up)
    above = lax.ppermute(piece, "ens", down)
    below, above, tables = lax.optimization_barrier((below, above, tables))
    far_first = lax.ppermute(below[:half], "ens", up)
    far_second = lax.ppermute(above[half:], "ens", down)
    near = place_near(places, piece, above, below, total)
    return (places, near, far_first, far_second), tables


def requests(dest_owner, dest_slot, held):
    owners = lax.axis_size("band")
    members = lax.axis_size("ens")
    total = dest_owner.size
    per_owner = total // owners
    quota = -(-per_owner // members)
    padded = -(-quota // 16) * 16
    columns = jnp.arange(total, dtype=jnp.int32)
    keys = (dest_owner * held + dest_slot).reshape(-1)
    keys, order = lax.sort((keys, columns), num_keys=1)
    slots = keys.reshape(owners, per_owner) - jnp.arange(owners, dtype=jnp.int32)[:, None] * held
    slots = jnp.pad(slots, ((0, 0), (0, quota * members - per_owner)))
    mine = lax.dynamic_slice_in_dim(slots, lax.axis_index("ens") * quota, quota, axis=1)
    mine = jnp.pad(mine, ((0, 0), (0, padded - quota)))
    return mine.reshape(owners, 1, padded), order


def places_of_rows(order, quota, longitudes):
    owners = lax.axis_size("band")
    members = lax.axis_size("ens")
    total = order.shape[0]
    per_owner = total // owners
    across = order % longitudes
    folded = jnp.where(across <= longitudes // 2, across, longitudes * 3 // 2 - across)
    order = order - across + folded
    places = jnp.pad(
        order.reshape(owners, per_owner),
        ((0, 0), (0, quota * members - per_owner)),
        constant_values=total,
    )
    places = places.reshape(owners, members, quota).transpose(1, 0, 2)
    places = jnp.concatenate([places, places], axis=0)
    places = lax.dynamic_slice_in_dim(places, lax.axis_index("ens"), members, axis=0)
    return places.reshape(members * owners, quota)


def local(
    spectral_state,
    lat_basis,
    quad_weight,
    wave_of_slot,
    dest_owner,
    dest_slot,
    surface,
    in_weight,
    surface_weight,
    in_bias,
    mid_weight,
    mid_bias,
    out_weight,
):
    bands = lax.axis_size("band")
    longitudes = dest_owner.shape[1]
    ids, order = requests(dest_owner, dest_slot, surface.shape[0])
    padded = ids.shape[2]
    quota = -(-(order.shape[0] // bands) // lax.axis_size("ens"))
    fourier = to_latitudes(lat_basis, spectral_state)
    replies = fetch_rows(exchange(ids), surface)
    replies, fourier = lax.optimization_barrier((replies, fourier))
    features = fourier.shape[1]
    fetched = exchange(replies.reshape(bands, padded, -1)).reshape(-1, surface.shape[1])
    places = places_of_rows(order, quota, longitudes)
    tables = fourier_tables(wave_of_slot, bands, longitudes)
    surface_rows, tables = gathered_over_members(places, fetched, order.shape[0], tables)
    banded = exchange(fourier.reshape(bands, -1, features)).reshape(-1, features)
    weight = quad_weight * math.sqrt(2.0 / longitudes)
    first = jnp.concatenate([in_weight, surface_weight], axis=0)
    network = (first, in_bias, mid_weight, mid_bias, out_weight)
    spectrum = column_spectrum(banded, tables, surface_rows, weight, bands, *network)
    owned = exchange(spectrum.reshape(bands, -1, features)).reshape(-1, features)
    return to_degrees(lat_basis, owned)


def solution(mesh):
    return jax.shard_map(
        local,
        mesh=mesh,
        in_specs=(
            P(("ens", "band"), None, None),
            P("band", None, None),
            P("band"),
            P(),
            P("band", None),
            P("band", None),
            P("band", None),
            P(),
            P(),
            P(),
            P(),
            P(),
            P(),
        ),
        out_specs=P(("ens", "band"), None, None),
        check_vma=False,
    )
```

```python
import functools
import math

import jax
import jax.numpy as jnp
from jax import lax
from jax.experimental import pallas as pl
from jax.experimental.pallas import tpu as pltpu
from jax.sharding import PartitionSpec as P

VMEM_BYTES = 24 * 1024 * 1024


def whole(shape):
    zeros = (0,) * len(shape)
    return pl.BlockSpec(shape, lambda *_: zeros)


def fourier_kernel(basis_ref, state_ref, out_ref, wide):
    slots, lats, features = pl.num_programs(0), basis_ref.shape[1], out_ref.shape[1]
    slot = pl.program_id(0)
    per_lat = out_ref.shape[0] // lats
    found = jnp.dot(basis_ref[0], state_ref[0], preferred_element_type=jnp.float32)
    for k in range(2):
        wide[pl.ds(2 * slot + k, lats, per_lat), :] = found[:, k * features : (k + 1) * features]

    @pl.when(slot == slots - 1)
    def _():
        out_ref[...] = wide[...].astype(out_ref.dtype)


def to_latitudes(lat_basis, spectral_state):
    slots, lats, degrees = lat_basis.shape
    features = spectral_state.shape[2] // 2
    rows = lats * slots * 2
    return pl.pallas_call(
        fourier_kernel,
        grid=(slots,),
        in_specs=[
            pl.BlockSpec((1, lats, degrees), lambda s: (s, 0, 0)),
            pl.BlockSpec((1, degrees, 2 * features), lambda s: (s, 0, 0)),
        ],
        out_specs=whole((rows, features)),
        out_shape=jax.ShapeDtypeStruct((rows, features), jnp.bfloat16),
        scratch_shapes=[pltpu.VMEM((rows, features), jnp.float32)],
        compiler_params=pltpu.CompilerParams(vmem_limit_bytes=VMEM_BYTES),
        cost_estimate=pl.CostEstimate(
            flops=2 * slots * lats * degrees * 2 * features,
            bytes_accessed=2 * (lat_basis.size + spectral_state.size + rows * features),
            transcendentals=0,
        ),
        name="to_latitudes",
    )(lat_basis, spectral_state)


def degrees_kernel(basis_ref, rows_ref, out_ref, wide):
    lats = basis_ref.shape[1]
    together = basis_ref.shape[0]
    step = pl.program_id(0)
    per_lat = rows_ref.shape[0] // lats

    @pl.when(step == 0)
    def _():
        wide[...] = rows_ref[...].astype(jnp.float32)

    for i in range(together):
        slot = step * together + i
        spectrum = jnp.concatenate(
            [wide[pl.ds(2 * slot + k, lats, per_lat), :].astype(jnp.bfloat16) for k in range(2)],
            axis=1,
        )
        out_ref[i] = lax.dot_general(
            basis_ref[i], spectrum, (((0,), (0,)), ((), ())), preferred_element_type=jnp.float32
        )


def to_degrees(lat_basis, rows):
    slots, lats, degrees = lat_basis.shape
    features = rows.shape[1]
    together = 2 if slots % 2 == 0 else 1
    return pl.pallas_call(
        degrees_kernel,
        grid=(slots // together,),
        in_specs=[
            pl.BlockSpec((together, lats, degrees), lambda s: (s, 0, 0)),
            pl.BlockSpec(memory_space=pltpu.VMEM),
        ],
        out_specs=pl.BlockSpec((together, degrees, 2 * features), lambda s: (s, 0, 0)),
        out_shape=jax.ShapeDtypeStruct((slots, degrees, 2 * features), jnp.float32),
        scratch_shapes=[pltpu.VMEM(rows.shape, jnp.float32)],
        compiler_params=pltpu.CompilerParams(vmem_limit_bytes=VMEM_BYTES),
        cost_estimate=pl.CostEstimate(
            flops=2 * slots * lats * degrees * 2 * features,
            bytes_accessed=2 * (lat_basis.size + rows.size) + 8 * slots * degrees * features,
            transcendentals=0,
        ),
        name="to_degrees",
    )(lat_basis, rows)


def angle_parts(waves, step, count, quarter, longitudes, axis):
    positions = jnp.arange(count, dtype=jnp.int32) * step
    shape = (-1, 1) if axis == 1 else (1, -1)
    phases = waves.reshape(shape) * positions.reshape(shape[::-1])
    phases = (phases + quarter.reshape(shape)) % longitudes
    angles = phases.astype(jnp.float32) * (2.0 * math.pi / longitudes)
    return jnp.cos(angles), jnp.sin(angles)


def table_kernel(hi_cos, hi_sin, lo_cos, lo_sin, hi_cos_t, hi_sin_t, lo_cos_t, lo_sin_t, out, out_t):
    longitudes = out.shape[1]
    width = lo_cos.shape[1]
    for a in range(hi_cos.shape[1]):
        size = min(width, longitudes - a * width)
        block = hi_cos[:, a : a + 1] * lo_cos[...] - hi_sin[:, a : a + 1] * lo_sin[...]
        out[:, a * width : a * width + size] = block[:, :size].astype(out.dtype)
    height = lo_cos_t.shape[0]
    for a in range(hi_cos_t.shape[0]):
        block = hi_cos_t[a : a + 1, :] * lo_cos_t[...] - hi_sin_t[a : a + 1, :] * lo_sin_t[...]
        out_t[a * height : (a + 1) * height, :] = block.astype(out_t.dtype)


def fourier_tables(wave_of_slot, sources, longitudes):
    per_source = wave_of_slot.shape[0] // sources
    waves = (wave_of_slot + 1).reshape(sources, per_source).T.reshape(-1)
    waves = jnp.concatenate([waves, waves])
    terms = waves.shape[0]
    quarter = jnp.arange(terms, dtype=jnp.int32) // (terms // 2) * (longitudes // 4)
    none = jnp.zeros_like(quarter)
    width, height = 128, 32
    kept = -(-(longitudes // 2 + 1) // height) * height
    wide = angle_parts(waves, width, -(-kept // width), quarter, longitudes, 1)
    wide += angle_parts(waves, 1, width, none, longitudes, 1)
    tall = angle_parts(waves, height, kept // height, quarter, longitudes, 0)
    tall += angle_parts(waves, 1, height, none, longitudes, 0)
    return pl.pallas_call(
        table_kernel,
        out_shape=(
            jax.ShapeDtypeStruct((terms, kept), jnp.bfloat16),
            jax.ShapeDtypeStruct((kept, terms), jnp.bfloat16),
        ),
        compiler_params=pltpu.CompilerParams(vmem_limit_bytes=VMEM_BYTES),
        cost_estimate=pl.CostEstimate(
            flops=6 * terms * kept, bytes_accessed=4 * terms * kept, transcendentals=0
        ),
        name="fourier_tables",
    )(*wide, *tall)


def silu(v):
    half = 0.5 * v
    return half + half * jnp.tanh(half)


def columns_kernel(
    sources,
    weight_ref,
    places_ref,
    far_first_ref,
    far_second_ref,
    rows_ref,
    table_ref,
    table_t_ref,
    near_ref,
    first_ref,
    first_bias_ref,
    mid_ref,
    mid_bias_ref,
    last_ref,
    out_ref,
    wide_in,
    wide_out,
    coefficients,
    evens,
    odds,
    far_full,
):
    step = pl.program_id(0)
    features = rows_ref.shape[1]
    terms = table_ref.shape[0] // sources
    kept = table_ref.shape[1]
    stride = rows_ref.shape[0] // sources
    lanes = coefficients.shape[1]
    group = lanes // features
    half = near_ref.shape[0] // group // 2
    split = table_ref.shape[0] // 2

    @pl.when(step == 0)
    def _():
        wide_in[...] = rows_ref[...].astype(jnp.float32)
        far_full[...] = jnp.zeros_like(far_full)
        far_half = far_first_ref.shape[0]
        far = wide_out.at[pl.ds(0, 2 * far_half)]
        far[:far_half, :] = far_first_ref[...].astype(jnp.float32)
        far[far_half:, :] = far_second_ref[...].astype(jnp.float32)
        owners = places_ref.shape[0] // 4
        padded = 2 * far_half // owners
        place_piece(places_ref, 2 * owners, places_ref.shape[1], padded, far, far_full)

    def place_of(q):
        return (q % 2) * split + q // 2 * sources

    for j in range(group):
        lat = step * group + j
        for q in range(terms):
            at = place_of(q)
            coefficients[at : at + sources, j * features : (j + 1) * features] = wide_in[
                pl.ds(terms * lat + q, sources, stride), :
            ].astype(jnp.bfloat16)

    def network(state, start):
        def surface_at(j):
            here = 2 * half * j + start
            at = pl.multiple_of(step * group * 2 * half + here, 16)
            near = near_ref[here : here + half, :].astype(jnp.float32)
            return (near + far_full[pl.ds(at, half), :]).astype(jnp.bfloat16)

        joined = jnp.concatenate(
            [
                jnp.concatenate(
                    [
                        state[:, j * features : (j + 1) * features].astype(jnp.bfloat16),
                        surface_at(j),
                    ],
                    axis=1,
                )
                for j in range(group)
            ],
            axis=0,
        )
        first = jnp.dot(joined, first_ref[...], preferred_element_type=jnp.float32)
        first = silu(first + first_bias_ref[...]).astype(jnp.bfloat16)
        second = jnp.dot(first, mid_ref[...], preferred_element_type=jnp.float32)
        second = silu(second + mid_bias_ref[...]).astype(jnp.bfloat16)
        third = jnp.dot(second, last_ref[...], preferred_element_type=jnp.float32)
        return jnp.concatenate([third[j * half : (j + 1) * half, :] for j in range(group)], axis=1)

    even = jnp.dot(
        table_t_ref[:, :split], coefficients[:split, :], preferred_element_type=jnp.float32
    )
    odd = jnp.dot(
        table_t_ref[:half, split:], coefficients[split:, :], preferred_element_type=jnp.float32
    )
    lone, even = even[half : half + 1, :], even[:half, :]
    top = lax.broadcasted_iota(jnp.int32, (half, lanes), 0) == 0
    east = network(even + odd, 0)
    west = network(jnp.where(top, lone, even - odd), half)
    evens[:half, :] = jnp.where(top, east, east + west).astype(jnp.bfloat16)
    evens[half:, :] = jnp.where(top[: kept - half, :], west[: kept - half, :], 0.0).astype(
        jnp.bfloat16
    )
    odds[:half, :] = (east - west).astype(jnp.bfloat16)
    odds[half:, :] = jnp.zeros((kept - half, lanes), jnp.bfloat16)

    for k, halves in enumerate((evens, odds)):
        spectrum = jnp.dot(
            table_ref[k * split : (k + 1) * split, :],
            halves[...],
            preferred_element_type=jnp.float32,
        )
        for j in range(group):
            lat = step * group + j
            scaled = spectrum[:, j * features : (j + 1) * features] * weight_ref[lat]
            for q in range(k, terms, 2):
                at = q // 2 * sources
                wide_out[pl.ds(terms * lat + q, sources, stride), :] = scaled[at : at + sources, :]

    @pl.when(step == pl.num_programs(0) - 1)
    def _():
        out_ref[...] = wide_out[...].astype(out_ref.dtype)


def column_spectrum(
    rows, tables, surface_rows, quad_weight, sources, first, first_bias, mid, mid_bias, last
):
    table, table_t = tables
    terms, kept = table.shape
    places, near, far_first, far_second = surface_rows
    longitudes = near.shape[0] // quad_weight.shape[0]
    features = rows.shape[1]
    lats = quad_weight.shape[0]
    group = 2 if lats % 2 == 0 else 1
    hidden = first.shape[1]
    columns = lats * longitudes
    flops = 2 * columns * (terms * features + 2 * features * hidden)
    flops += 2 * columns * (hidden * hidden + hidden * features)
    return pl.pallas_call(
        functools.partial(columns_kernel, sources),
        grid=(lats // group,),
        in_specs=[
            pl.BlockSpec(memory_space=pltpu.SMEM),
            pl.BlockSpec(memory_space=pltpu.SMEM),
            whole(far_first.shape),
            whole(far_second.shape),
            whole(rows.shape),
            whole(table.shape),
            whole(table_t.shape),
            pl.BlockSpec((group * longitudes, near.shape[1]), lambda i: (i, 0)),
            whole(first.shape),
            whole((1, hidden)),
            whole(mid.shape),
            whole((1, hidden)),
            whole(last.shape),
        ],
        out_specs=whole(rows.shape),
        out_shape=jax.ShapeDtypeStruct(rows.shape, jnp.bfloat16),
        scratch_shapes=[
            pltpu.VMEM(rows.shape, jnp.float32),
            pltpu.VMEM(rows.shape, jnp.float32),
            pltpu.VMEM((terms, group * features), jnp.bfloat16),
            pltpu.VMEM((kept, group * features), jnp.bfloat16),
            pltpu.VMEM((kept, group * features), jnp.bfloat16),
            pltpu.VMEM((near.shape[0] + 8, near.shape[1]), jnp.float32),
        ],
        compiler_params=pltpu.CompilerParams(vmem_limit_bytes=60 * 1024 * 1024),
        cost_estimate=pl.CostEstimate(
            flops=flops,
            bytes_accessed=2 * (2 * rows.size + 2 * table.size + near.size),
            transcendentals=2 * columns * hidden,
        ),
        name="column_spectrum",
    )(
        quad_weight,
        places,
        far_first,
        far_second,
        rows,
        table,
        table_t,
        near,
        first,
        first_bias.reshape(1, hidden),
        mid,
        mid_bias.reshape(1, hidden),
        last,
    )


def exchange(chunks):
    return lax.all_to_all(chunks, "band", split_axis=0, concat_axis=0, tiled=True)


def fetch_kernel(ids_ref, held_ref, out_ref, wide, found):
    wide[...] = held_ref[...].astype(jnp.float32)
    count = ids_ref.shape[2]

    def one_peer(peer, carry):
        base = pl.multiple_of(peer * count, count)
        for i in range(count):
            found[pl.ds(base + i, 1), :] = wide[pl.ds(ids_ref[peer, 0, i], 1), :]
        return carry

    lax.fori_loop(0, ids_ref.shape[0], one_peer, 0)
    out_ref[...] = found[...].astype(out_ref.dtype)


def fetch_rows(ids, held):
    rows = ids.shape[0] * ids.shape[2]
    features = held.shape[1]
    return pl.pallas_call(
        fetch_kernel,
        in_specs=[pl.BlockSpec(memory_space=pltpu.SMEM), pl.BlockSpec(memory_space=pltpu.VMEM)],
        out_specs=pl.BlockSpec(memory_space=pltpu.VMEM),
        out_shape=jax.ShapeDtypeStruct((rows, features), held.dtype),
        scratch_shapes=[
            pltpu.VMEM(held.shape, jnp.float32),
            pltpu.VMEM((rows, features), jnp.float32),
        ],
        compiler_params=pltpu.CompilerParams(vmem_limit_bytes=VMEM_BYTES),
        cost_estimate=pl.CostEstimate(
            flops=0, bytes_accessed=20 * 2 * (held.size + rows * features), transcendentals=0
        ),
        name="fetch_rows",
    )(ids, held)


def place_piece(places_ref, first, quota, padded, wide, full_ref):
    def one_owner(owner, carry):
        base = pl.multiple_of(owner * padded, padded)
        for i in range(quota):
            full_ref[pl.ds(places_ref[first + owner, i], 1), :] = wide[pl.ds(base + i, 1), :]
        return carry

    lax.fori_loop(0, wide.shape[0] // padded, one_owner, 0)


def near_kernel(
    padded, places_ref, own_ref, above_a, above_b, below_a, below_b, out_ref, full, wide
):
    owners = wide.shape[0] // padded
    full[...] = jnp.zeros_like(full)
    for away, pieces in ((0, (own_ref,)), (1, (above_a, above_b)), (3, (below_a, below_b))):
        at = 0
        for piece in pieces:
            wide[at : at + piece.shape[0], :] = piece[...].astype(jnp.float32)
            at += piece.shape[0]
        place_piece(places_ref, away * owners, places_ref.shape[1], padded, wide, full)
    out_ref[...] = full[: out_ref.shape[0], :].astype(out_ref.dtype)


def place_near(places, own, others, total):
    padded = own.shape[0] // (places.shape[0] // 4)
    features = own.shape[1]
    return pl.pallas_call(
        functools.partial(near_kernel, padded),
        in_specs=[pl.BlockSpec(memory_space=pltpu.SMEM)]
        + [pl.BlockSpec(memory_space=pltpu.VMEM)] * 5,
        out_specs=pl.BlockSpec(memory_space=pltpu.VMEM),
        out_shape=jax.ShapeDtypeStruct((total, features), own.dtype),
        scratch_shapes=[
            pltpu.VMEM((total + 8, features), jnp.float32),
            pltpu.VMEM(own.shape, jnp.float32),
        ],
        compiler_params=pltpu.CompilerParams(vmem_limit_bytes=VMEM_BYTES),
        cost_estimate=pl.CostEstimate(flops=0, bytes_accessed=30 * 2**20, transcendentals=0),
        name="place_near",
    )(places, own, *others)


def gathered_over_members(places, piece, total, tables):
    members = lax.axis_size("ens")
    up = [(i, (i + 1) % members) for i in range(members)]
    down = [(i, (i - 1) % members) for i in range(members)]
    half = piece.shape[0] // 2
    first, second = piece[:half], piece[half:]
    below_a = lax.ppermute(first, "ens", up)
    above_b = lax.ppermute(second, "ens", down)
    below_b = lax.ppermute(second, "ens", up)
    above_a = lax.ppermute(first, "ens", down)
    far_a = lax.ppermute(below_a, "ens", up)
    far_b = lax.ppermute(above_b, "ens", down)
    below_b, above_a, tables = lax.optimization_barrier((below_b, above_a, tables))
    near = place_near(places, piece, (above_a, above_b, below_a, below_b), total)
    return (places, near, far_a, far_b), tables


def requests(dest_owner, dest_slot, held):
    owners = lax.axis_size("band")
    members = lax.axis_size("ens")
    total = dest_owner.size
    per_owner = total // owners
    quota = -(-per_owner // members)
    padded = -(-quota // 16) * 16
    columns = jnp.arange(total, dtype=jnp.int32)
    keys = (dest_owner * held + dest_slot).reshape(-1)
    keys, order = lax.sort((keys, columns), num_keys=1)
    slots = keys.reshape(owners, per_owner) - jnp.arange(owners, dtype=jnp.int32)[:, None] * held
    slots = jnp.pad(slots, ((0, 0), (0, quota * members - per_owner)))
    mine = lax.dynamic_slice_in_dim(slots, lax.axis_index("ens") * quota, quota, axis=1)
    mine = jnp.pad(mine, ((0, 0), (0, padded - quota)))
    return mine.reshape(owners, 1, padded), order


def places_of_rows(order, quota, longitudes):
    owners = lax.axis_size("band")
    members = lax.axis_size("ens")
    total = order.shape[0]
    per_owner = total // owners
    across = order % longitudes
    folded = jnp.where(across <= longitudes // 2, across, longitudes * 3 // 2 - across)
    order = order - across + folded
    places = jnp.pad(
        order.reshape(owners, per_owner),
        ((0, 0), (0, quota * members - per_owner)),
        constant_values=total,
    )
    places = places.reshape(owners, members, quota).transpose(1, 0, 2)
    places = jnp.concatenate([places, places], axis=0)
    places = lax.dynamic_slice_in_dim(places, lax.axis_index("ens"), members, axis=0)
    return places.reshape(members * owners, quota)


def local(
    spectral_state,
    lat_basis,
    quad_weight,
    wave_of_slot,
    dest_owner,
    dest_slot,
    surface,
    in_weight,
    surface_weight,
    in_bias,
    mid_weight,
    mid_bias,
    out_weight,
):
    bands = lax.axis_size("band")
    longitudes = dest_owner.shape[1]
    ids, order = requests(dest_owner, dest_slot, surface.shape[0])
    padded = ids.shape[2]
    quota = -(-(order.shape[0] // bands) // lax.axis_size("ens"))
    fourier = to_latitudes(lat_basis, spectral_state)
    replies = fetch_rows(exchange(ids), surface)
    replies, fourier = lax.optimization_barrier((replies, fourier))
    features = fourier.shape[1]
    fetched = exchange(replies.reshape(bands, padded, -1)).reshape(-1, surface.shape[1])
    places = places_of_rows(order, quota, longitudes)
    tables = fourier_tables(wave_of_slot, bands, longitudes)
    surface_rows, tables = gathered_over_members(places, fetched, order.shape[0], tables)
    banded = exchange(fourier.reshape(bands, -1, features)).reshape(-1, features)
    weight = quad_weight * math.sqrt(2.0 / longitudes)
    first = jnp.concatenate([in_weight, surface_weight], axis=0)
    network = (first, in_bias, mid_weight, mid_bias, out_weight)
    spectrum = column_spectrum(banded, tables, surface_rows, weight, bands, *network)
    owned = exchange(spectrum.reshape(bands, -1, features)).reshape(-1, features)
    return to_degrees(lat_basis, owned)


def solution(mesh):
    return jax.shard_map(
        local,
        mesh=mesh,
        in_specs=(
            P(("ens", "band"), None, None),
            P("band", None, None),
            P("band"),
            P(),
            P("band", None),
            P("band", None),
            P("band", None),
            P(),
            P(),
            P(),
            P(),
            P(),
            P(),
        ),
        out_specs=P(("ens", "band"), None, None),
        check_vma=False,
    )
```

```python
import functools
import math

import jax
import jax.numpy as jnp
from jax import lax
from jax.experimental import pallas as pl
from jax.experimental.pallas import tpu as pltpu
from jax.sharding import PartitionSpec as P

VMEM_BYTES = 24 * 1024 * 1024


def whole(shape):
    zeros = (0,) * len(shape)
    return pl.BlockSpec(shape, lambda *_: zeros)


def fourier_kernel(basis_ref, state_ref, out_ref, wide):
    slots, lats, features = pl.num_programs(0), basis_ref.shape[1], out_ref.shape[1]
    slot = pl.program_id(0)
    per_lat = out_ref.shape[0] // lats
    found = jnp.dot(basis_ref[0], state_ref[0], preferred_element_type=jnp.float32)
    for k in range(2):
        wide[pl.ds(2 * slot + k, lats, per_lat), :] = found[:, k * features : (k + 1) * features]

    @pl.when(slot == slots - 1)
    def _():
        out_ref[...] = wide[...].astype(out_ref.dtype)


def to_latitudes(lat_basis, spectral_state):
    slots, lats, degrees = lat_basis.shape
    features = spectral_state.shape[2] // 2
    rows = lats * slots * 2
    return pl.pallas_call(
        fourier_kernel,
        grid=(slots,),
        in_specs=[
            pl.BlockSpec((1, lats, degrees), lambda s: (s, 0, 0)),
            pl.BlockSpec((1, degrees, 2 * features), lambda s: (s, 0, 0)),
        ],
        out_specs=whole((rows, features)),
        out_shape=jax.ShapeDtypeStruct((rows, features), jnp.bfloat16),
        scratch_shapes=[pltpu.VMEM((rows, features), jnp.float32)],
        compiler_params=pltpu.CompilerParams(vmem_limit_bytes=VMEM_BYTES),
        cost_estimate=pl.CostEstimate(
            flops=2 * slots * lats * degrees * 2 * features,
            bytes_accessed=2 * (lat_basis.size + spectral_state.size + rows * features),
            transcendentals=0,
        ),
        name="to_latitudes",
    )(lat_basis, spectral_state)


def degrees_kernel(basis_ref, rows_ref, out_ref, wide):
    lats = basis_ref.shape[1]
    together = basis_ref.shape[0]
    step = pl.program_id(0)
    per_lat = rows_ref.shape[0] // lats

    @pl.when(step == 0)
    def _():
        wide[...] = rows_ref[...].astype(jnp.float32)

    for i in range(together):
        slot = step * together + i
        spectrum = jnp.concatenate(
            [wide[pl.ds(2 * slot + k, lats, per_lat), :].astype(jnp.bfloat16) for k in range(2)],
            axis=1,
        )
        out_ref[i] = lax.dot_general(
            basis_ref[i], spectrum, (((0,), (0,)), ((), ())), preferred_element_type=jnp.float32
        )


def to_degrees(lat_basis, rows):
    slots, lats, degrees = lat_basis.shape
    features = rows.shape[1]
    together = 3 if slots % 3 == 0 else 1
    return pl.pallas_call(
        degrees_kernel,
        grid=(slots // together,),
        in_specs=[
            pl.BlockSpec((together, lats, degrees), lambda s: (s, 0, 0)),
            pl.BlockSpec(memory_space=pltpu.VMEM),
        ],
        out_specs=pl.BlockSpec((together, degrees, 2 * features), lambda s: (s, 0, 0)),
        out_shape=jax.ShapeDtypeStruct((slots, degrees, 2 * features), jnp.float32),
        scratch_shapes=[pltpu.VMEM(rows.shape, jnp.float32)],
        compiler_params=pltpu.CompilerParams(vmem_limit_bytes=VMEM_BYTES),
        cost_estimate=pl.CostEstimate(
            flops=2 * slots * lats * degrees * 2 * features,
            bytes_accessed=2 * (lat_basis.size + rows.size) + 8 * slots * degrees * features,
            transcendentals=0,
        ),
        name="to_degrees",
    )(lat_basis, rows)


def angle_parts(waves, step, count, quarter, longitudes, axis):
    positions = jnp.arange(count, dtype=jnp.int32) * step
    shape = (-1, 1) if axis == 1 else (1, -1)
    phases = waves.reshape(shape) * positions.reshape(shape[::-1])
    phases = (phases + quarter.reshape(shape)) % longitudes
    angles = phases.astype(jnp.float32) * (2.0 * math.pi / longitudes)
    return jnp.cos(angles), jnp.sin(angles)


def table_kernel(hi_cos, hi_sin, lo_cos, lo_sin, hi_cos_t, hi_sin_t, lo_cos_t, lo_sin_t, out, out_t):
    longitudes = out.shape[1]
    width = lo_cos.shape[1]
    for a in range(hi_cos.shape[1]):
        size = min(width, longitudes - a * width)
        block = hi_cos[:, a : a + 1] * lo_cos[...] - hi_sin[:, a : a + 1] * lo_sin[...]
        out[:, a * width : a * width + size] = block[:, :size].astype(out.dtype)
    height = lo_cos_t.shape[0]
    for a in range(hi_cos_t.shape[0]):
        block = hi_cos_t[a : a + 1, :] * lo_cos_t[...] - hi_sin_t[a : a + 1, :] * lo_sin_t[...]
        out_t[a * height : (a + 1) * height, :] = block.astype(out_t.dtype)


def fourier_tables(wave_of_slot, sources, longitudes):
    per_source = wave_of_slot.shape[0] // sources
    waves = (wave_of_slot + 1).reshape(sources, per_source).T.reshape(-1)
    waves = jnp.concatenate([waves, waves])
    terms = waves.shape[0]
    quarter = jnp.arange(terms, dtype=jnp.int32) // (terms // 2) * (longitudes // 4)
    none = jnp.zeros_like(quarter)
    width, height = 128, 32
    kept = -(-(longitudes // 2 + 1) // height) * height
    wide = angle_parts(waves, width, -(-kept // width), quarter, longitudes, 1)
    wide += angle_parts(waves, 1, width, none, longitudes, 1)
    tall = angle_parts(waves, height, kept // height, quarter, longitudes, 0)
    tall += angle_parts(waves, 1, height, none, longitudes, 0)
    return pl.pallas_call(
        table_kernel,
        out_shape=(
            jax.ShapeDtypeStruct((terms, kept), jnp.bfloat16),
            jax.ShapeDtypeStruct((kept, terms), jnp.bfloat16),
        ),
        compiler_params=pltpu.CompilerParams(vmem_limit_bytes=VMEM_BYTES),
        cost_estimate=pl.CostEstimate(
            flops=6 * terms * kept, bytes_accessed=4 * terms * kept, transcendentals=0
        ),
        name="fourier_tables",
    )(*wide, *tall)


def silu(v):
    half = 0.5 * v
    return half + half * jnp.tanh(half)


def columns_kernel(
    sources,
    weight_ref,
    places_ref,
    far_first_ref,
    far_second_ref,
    rows_ref,
    table_ref,
    table_t_ref,
    near_ref,
    first_ref,
    first_bias_ref,
    mid_ref,
    mid_bias_ref,
    last_ref,
    out_ref,
    wide_in,
    wide_out,
    coefficients,
    evens,
    odds,
    far_full,
):
    step = pl.program_id(0)
    features = rows_ref.shape[1]
    terms = table_ref.shape[0] // sources
    kept = table_ref.shape[1]
    stride = rows_ref.shape[0] // sources
    lanes = coefficients.shape[1]
    group = lanes // features
    half = near_ref.shape[0] // group // 2
    split = table_ref.shape[0] // 2

    @pl.when(step == 0)
    def _():
        wide_in[...] = rows_ref[...].astype(jnp.float32)
        far_full[...] = jnp.zeros_like(far_full)
        far_half = far_first_ref.shape[0]
        far = wide_out.at[pl.ds(0, 2 * far_half)]
        far[:far_half, :] = far_first_ref[...].astype(jnp.float32)
        far[far_half:, :] = far_second_ref[...].astype(jnp.float32)
        owners = places_ref.shape[0] // 4
        padded = 2 * far_half // owners
        place_piece(places_ref, 2 * owners, places_ref.shape[1], padded, far, far_full)

    def place_of(q):
        return (q % 2) * split + q // 2 * sources

    for j in range(group):
        lat = step * group + j
        for q in range(terms):
            at = place_of(q)
            coefficients[at : at + sources, j * features : (j + 1) * features] = wide_in[
                pl.ds(terms * lat + q, sources, stride), :
            ].astype(jnp.bfloat16)

    def network(state, start):
        def surface_at(j):
            here = 2 * half * j + start
            at = pl.multiple_of(step * group * 2 * half + here, 16)
            near = near_ref[here : here + half, :].astype(jnp.float32)
            return (near + far_full[pl.ds(at, half), :]).astype(jnp.bfloat16)

        joined = jnp.concatenate(
            [
                jnp.concatenate(
                    [
                        state[:, j * features : (j + 1) * features].astype(jnp.bfloat16),
                        surface_at(j),
                    ],
                    axis=1,
                )
                for j in range(group)
            ],
            axis=0,
        )
        first = jnp.dot(joined, first_ref[...], preferred_element_type=jnp.float32)
        first = silu(first + first_bias_ref[...]).astype(jnp.bfloat16)
        second = jnp.dot(first, mid_ref[...], preferred_element_type=jnp.float32)
        second = silu(second + mid_bias_ref[...]).astype(jnp.bfloat16)
        third = jnp.dot(second, last_ref[...], preferred_element_type=jnp.float32)
        return jnp.concatenate([third[j * half : (j + 1) * half, :] for j in range(group)], axis=1)

    even = jnp.dot(
        table_t_ref[:, :split], coefficients[:split, :], preferred_element_type=jnp.float32
    )
    odd = jnp.dot(
        table_t_ref[:half, split:], coefficients[split:, :], preferred_element_type=jnp.float32
    )
    lone, even = even[half : half + 1, :], even[:half, :]
    top = lax.broadcasted_iota(jnp.int32, (half, lanes), 0) == 0
    east = network(even + odd, 0)
    west = network(jnp.where(top, lone, even - odd), half)
    evens[:half, :] = jnp.where(top, east, east + west).astype(jnp.bfloat16)
    evens[half:, :] = jnp.where(top[: kept - half, :], west[: kept - half, :], 0.0).astype(
        jnp.bfloat16
    )
    odds[:half, :] = (east - west).astype(jnp.bfloat16)
    odds[half:, :] = jnp.zeros((kept - half, lanes), jnp.bfloat16)

    for k, halves in enumerate((evens, odds)):
        spectrum = jnp.dot(
            table_ref[k * split : (k + 1) * split, :],
            halves[...],
            preferred_element_type=jnp.float32,
        )
        for j in range(group):
            lat = step * group + j
            scaled = spectrum[:, j * features : (j + 1) * features] * weight_ref[lat]
            for q in range(k, terms, 2):
                at = q // 2 * sources
                wide_out[pl.ds(terms * lat + q, sources, stride), :] = scaled[at : at + sources, :]

    @pl.when(step == pl.num_programs(0) - 1)
    def _():
        out_ref[...] = wide_out[...].astype(out_ref.dtype)


def column_spectrum(
    rows, tables, surface_rows, quad_weight, sources, first, first_bias, mid, mid_bias, last
):
    table, table_t = tables
    terms, kept = table.shape
    places, near, far_first, far_second = surface_rows
    longitudes = near.shape[0] // quad_weight.shape[0]
    features = rows.shape[1]
    lats = quad_weight.shape[0]
    group = 2 if lats % 2 == 0 else 1
    hidden = first.shape[1]
    columns = lats * longitudes
    flops = 2 * columns * (terms * features + 2 * features * hidden)
    flops += 2 * columns * (hidden * hidden + hidden * features)
    return pl.pallas_call(
        functools.partial(columns_kernel, sources),
        grid=(lats // group,),
        in_specs=[
            pl.BlockSpec(memory_space=pltpu.SMEM),
            pl.BlockSpec(memory_space=pltpu.SMEM),
            whole(far_first.shape),
            whole(far_second.shape),
            whole(rows.shape),
            whole(table.shape),
            whole(table_t.shape),
            pl.BlockSpec((group * longitudes, near.shape[1]), lambda i: (i, 0)),
            whole(first.shape),
            whole((1, hidden)),
            whole(mid.shape),
            whole((1, hidden)),
            whole(last.shape),
        ],
        out_specs=whole(rows.shape),
        out_shape=jax.ShapeDtypeStruct(rows.shape, jnp.bfloat16),
        scratch_shapes=[
            pltpu.VMEM(rows.shape, jnp.float32),
            pltpu.VMEM(rows.shape, jnp.float32),
            pltpu.VMEM((terms, group * features), jnp.bfloat16),
            pltpu.VMEM((kept, group * features), jnp.bfloat16),
            pltpu.VMEM((kept, group * features), jnp.bfloat16),
            pltpu.VMEM((near.shape[0] + 8, near.shape[1]), jnp.float32),
        ],
        compiler_params=pltpu.CompilerParams(vmem_limit_bytes=60 * 1024 * 1024),
        cost_estimate=pl.CostEstimate(
            flops=flops,
            bytes_accessed=2 * (2 * rows.size + 2 * table.size + near.size),
            transcendentals=2 * columns * hidden,
        ),
        name="column_spectrum",
    )(
        quad_weight,
        places,
        far_first,
        far_second,
        rows,
        table,
        table_t,
        near,
        first,
        first_bias.reshape(1, hidden),
        mid,
        mid_bias.reshape(1, hidden),
        last,
    )


def exchange(chunks):
    return lax.all_to_all(chunks, "band", split_axis=0, concat_axis=0, tiled=True)


def fetch_kernel(ids_ref, held_ref, out_ref, wide, found):
    wide[...] = held_ref[...].astype(jnp.float32)
    count = ids_ref.shape[2]

    def one_peer(peer, carry):
        base = pl.multiple_of(peer * count, count)
        for i in range(count):
            found[pl.ds(base + i, 1), :] = wide[pl.ds(ids_ref[peer, 0, i], 1), :]
        return carry

    lax.fori_loop(0, ids_ref.shape[0], one_peer, 0)
    out_ref[...] = found[...].astype(out_ref.dtype)


def fetch_rows(ids, held):
    rows = ids.shape[0] * ids.shape[2]
    features = held.shape[1]
    return pl.pallas_call(
        fetch_kernel,
        in_specs=[pl.BlockSpec(memory_space=pltpu.SMEM), pl.BlockSpec(memory_space=pltpu.VMEM)],
        out_specs=pl.BlockSpec(memory_space=pltpu.VMEM),
        out_shape=jax.ShapeDtypeStruct((rows, features), held.dtype),
        scratch_shapes=[
            pltpu.VMEM(held.shape, jnp.float32),
            pltpu.VMEM((rows, features), jnp.float32),
        ],
        compiler_params=pltpu.CompilerParams(vmem_limit_bytes=VMEM_BYTES),
        cost_estimate=pl.CostEstimate(
            flops=0, bytes_accessed=20 * 2 * (held.size + rows * features), transcendentals=0
        ),
        name="fetch_rows",
    )(ids, held)


def place_piece(places_ref, first, quota, padded, wide, full_ref):
    def one_owner(owner, carry):
        base = pl.multiple_of(owner * padded, padded)
        for i in range(quota):
            full_ref[pl.ds(places_ref[first + owner, i], 1), :] = wide[pl.ds(base + i, 1), :]
        return carry

    lax.fori_loop(0, wide.shape[0] // padded, one_owner, 0)


def near_kernel(
    padded, places_ref, own_ref, above_a, above_b, below_a, below_b, out_ref, full, wide
):
    owners = wide.shape[0] // padded
    full[...] = jnp.zeros_like(full)
    for away, pieces in ((0, (own_ref,)), (1, (above_a, above_b)), (3, (below_a, below_b))):
        at = 0
        for piece in pieces:
            wide[at : at + piece.shape[0], :] = piece[...].astype(jnp.float32)
            at += piece.shape[0]
        place_piece(places_ref, away * owners, places_ref.shape[1], padded, wide, full)
    out_ref[...] = full[: out_ref.shape[0], :].astype(out_ref.dtype)


def place_near(places, own, others, total):
    padded = own.shape[0] // (places.shape[0] // 4)
    features = own.shape[1]
    return pl.pallas_call(
        functools.partial(near_kernel, padded),
        in_specs=[pl.BlockSpec(memory_space=pltpu.SMEM)]
        + [pl.BlockSpec(memory_space=pltpu.VMEM)] * 5,
        out_specs=pl.BlockSpec(memory_space=pltpu.VMEM),
        out_shape=jax.ShapeDtypeStruct((total, features), own.dtype),
        scratch_shapes=[
            pltpu.VMEM((total + 8, features), jnp.float32),
            pltpu.VMEM(own.shape, jnp.float32),
        ],
        compiler_params=pltpu.CompilerParams(vmem_limit_bytes=VMEM_BYTES),
        cost_estimate=pl.CostEstimate(flops=0, bytes_accessed=30 * 2**20, transcendentals=0),
        name="place_near",
    )(places, own, *others)


def gathered_over_members(places, piece, total, tables):
    members = lax.axis_size("ens")
    up = [(i, (i + 1) % members) for i in range(members)]
    down = [(i, (i - 1) % members) for i in range(members)]
    half = piece.shape[0] // 2
    first, second = piece[:half], piece[half:]
    below_a = lax.ppermute(first, "ens", up)
    above_b = lax.ppermute(second, "ens", down)
    below_b = lax.ppermute(second, "ens", up)
    above_a = lax.ppermute(first, "ens", down)
    far_a = lax.ppermute(below_a, "ens", up)
    far_b = lax.ppermute(above_b, "ens", down)
    below_b, above_a, tables = lax.optimization_barrier((below_b, above_a, tables))
    near = place_near(places, piece, (above_a, above_b, below_a, below_b), total)
    return (places, near, far_a, far_b), tables


def requests(dest_owner, dest_slot, held):
    owners = lax.axis_size("band")
    members = lax.axis_size("ens")
    total = dest_owner.size
    per_owner = total // owners
    quota = -(-per_owner // members)
    padded = -(-quota // 16) * 16
    columns = jnp.arange(total, dtype=jnp.int32)
    keys = (dest_owner * held + dest_slot).reshape(-1)
    keys, order = lax.sort((keys, columns), num_keys=1)
    slots = keys.reshape(owners, per_owner) - jnp.arange(owners, dtype=jnp.int32)[:, None] * held
    slots = jnp.pad(slots, ((0, 0), (0, quota * members - per_owner)))
    mine = lax.dynamic_slice_in_dim(slots, lax.axis_index("ens") * quota, quota, axis=1)
    mine = jnp.pad(mine, ((0, 0), (0, padded - quota)))
    return mine.reshape(owners, 1, padded), order


def places_of_rows(order, quota, longitudes):
    owners = lax.axis_size("band")
    members = lax.axis_size("ens")
    total = order.shape[0]
    per_owner = total // owners
    across = order % longitudes
    folded = jnp.where(across <= longitudes // 2, across, longitudes * 3 // 2 - across)
    order = order - across + folded
    places = jnp.pad(
        order.reshape(owners, per_owner),
        ((0, 0), (0, quota * members - per_owner)),
        constant_values=total,
    )
    places = places.reshape(owners, members, quota).transpose(1, 0, 2)
    places = jnp.concatenate([places, places], axis=0)
    places = lax.dynamic_slice_in_dim(places, lax.axis_index("ens"), members, axis=0)
    return places.reshape(members * owners, quota)


def local(
    spectral_state,
    lat_basis,
    quad_weight,
    wave_of_slot,
    dest_owner,
    dest_slot,
    surface,
    in_weight,
    surface_weight,
    in_bias,
    mid_weight,
    mid_bias,
    out_weight,
):
    bands = lax.axis_size("band")
    longitudes = dest_owner.shape[1]
    ids, order = requests(dest_owner, dest_slot, surface.shape[0])
    padded = ids.shape[2]
    quota = -(-(order.shape[0] // bands) // lax.axis_size("ens"))
    fourier = to_latitudes(lat_basis, spectral_state)
    replies = fetch_rows(exchange(ids), surface)
    replies, fourier = lax.optimization_barrier((replies, fourier))
    features = fourier.shape[1]
    fetched = exchange(replies.reshape(bands, padded, -1)).reshape(-1, surface.shape[1])
    places = places_of_rows(order, quota, longitudes)
    tables = fourier_tables(wave_of_slot, bands, longitudes)
    surface_rows, tables = gathered_over_members(places, fetched, order.shape[0], tables)
    banded = exchange(fourier.reshape(bands, -1, features)).reshape(-1, features)
    weight = quad_weight * math.sqrt(2.0 / longitudes)
    first = jnp.concatenate([in_weight, surface_weight], axis=0)
    network = (first, in_bias, mid_weight, mid_bias, out_weight)
    spectrum = column_spectrum(banded, tables, surface_rows, weight, bands, *network)
    owned = exchange(spectrum.reshape(bands, -1, features)).reshape(-1, features)
    return to_degrees(lat_basis, owned)


def solution(mesh):
    return jax.shard_map(
        local,
        mesh=mesh,
        in_specs=(
            P(("ens", "band"), None, None),
            P("band", None, None),
            P("band"),
            P(),
            P("band", None),
            P("band", None),
            P("band", None),
            P(),
            P(),
            P(),
            P(),
            P(),
            P(),
        ),
        out_specs=P(("ens", "band"), None, None),
        check_vma=False,
    )
```
